32 devices in a mesh: gx: 4 (over z), gy: 2 (over y), af: 4 (over x, core).
Axes of the slice: x: 2, y: 2, z: 4, core: 2. Of those that a mesh axis runs over, the one named last changes fastest.
Arguments:
- electric: float32 [3, 64, 16, 512], P(None, 'gx', 'gy', 'af'), may hold values from -6 to 6
- material: int32 [64, 16, 512], P('gx', 'gy', 'af'), may hold values from 0 to 15
- coef_keep: float32 [3, 16], replicated, may hold values from 0.6 to 1
- coef_curl: float32 [3, 16], replicated, may hold values from 0.1 to 0.5
- huygens_count: int32 [4, 2, 4], P('gx', 'gy', 'af'), may hold values from 1 to 512, as said below
- huygens_cells: int32 [4, 2, 4, 512], P('gx', 'gy', 'af'), may hold values from 0 to 16383
- band_tiles: int32 [8, 8, 4], P(('gx', 'gy'), 'af'), may hold values from 0 to 15, as said below
- radiation: bfloat16 [8, 8, 4, 6, 128, 128], P('af', ('gx', 'gy')), may hold values from -0.0390625 to 0.0390625
Outputs:
- electric_end: float32 [3, 64, 16, 512], P(None, 'gx', 'gy', 'af')
- magnetic_end: float32 [3, 64, 16, 512], P(None, 'gx', 'gy', 'af')
- pattern: float32 [4, 1024], P(None, 'af')
The draws below stay inside these ranges and needn't reach their ends.
Inputs may be any that keep to these rules, and one draw needn't show every extreme that they name: `huygens_count`: every brick has 1 to 512 live rows, and some brick has exactly 512. `band_tiles`: the 4 tiles of one group and direction block are distinct, and every tile of a group is listed by some direction block.
All inputs are finite; a program needn't handle non-finite values.
Results may differ from the reference program's by a relative error of at most 0.0029.
Values may be sent and summed in bfloat16 or wider, within the bound.
A program may use at most 64 MiB of HBM per device.

```python
import jax
import jax.numpy as jnp
from jax import lax

CX = 16
CY = 8
CZ = 128
STEPS = 4
MATS = 16
NDIR = 1024
NDB = 8
RT = 128
TPB = 4
NBAND = 4
DB = 128
HMAX = 512
BRX = 4
BRY = 2
BRZ = 4
GROUPS = 8
NX = 64
NY = 16
NZ = 512
KFAN = 24576


def draw_huygens_count(key, part):
    bricks = BRX * BRY * BRZ
    counts = jax.random.randint(jax.random.fold_in(key, 11), (bricks,), 1, HMAX + 1)
    chosen = jax.random.randint(jax.random.fold_in(key, 12), (), 0, bricks)
    flattened = jnp.where(jnp.arange(bricks) == chosen, HMAX, counts)
    return flattened.reshape(BRX, BRY, BRZ).astype(jnp.int32)


def draw_band_tiles(key, part):
    ntiles = BRZ * TPB

    def shuffle(subkey):
        return jax.random.permutation(subkey, ntiles)
    subkeys = jax.random.split(jax.random.fold_in(key, 21), GROUPS)
    orders = jax.vmap(shuffle)(subkeys)
    positions = (jnp.arange(NDB)[:, None] * NBAND + jnp.arange(NBAND)[None, :]) % ntiles
    return orders[:, positions].astype(jnp.int32)


def place_ends(entries, stream_key, low, largest):
    longest = entries.shape.index(max(entries.shape))
    spots = []
    for shift in (0, 1):
        where = [jax.random.randint(jax.random.fold_in(stream_key, axis), (), 0, length) for axis, length in enumerate(entries.shape)]
        where[longest] = (where[longest] + shift) % entries.shape[longest]
        spots.append(tuple(where))
    return entries.at[spots[0]].set(low).at[spots[1]].set(largest)


def level_of(stream_key, dims, cuts, low, top_value):
    level = 1.0
    for dim, shards_of in cuts:
        draws = jax.random.uniform(jax.random.fold_in(jax.random.fold_in(stream_key, 6), dim), (shards_of,), jnp.float32, low / len(cuts), top_value / len(cuts))
        level = level * jnp.repeat(jnp.exp(draws), dims[dim] // shards_of).reshape((-1,) + (1,) * (len(dims) - 1 - dim))
    return level


def gaussian(own_key, dims, scale, bound, cuts=(), held_as=jnp.bfloat16):
    drawn = jax.random.normal(own_key, dims, jnp.float32) * scale
    if len(cuts) > 0:
        drawn = level_of(own_key, dims, cuts, -0.22, 0.18) * drawn
    return jnp.clip(drawn, min=-bound, max=bound).astype(held_as)


def setup_inputs(seed: int = 0) -> dict:
    splits = jax.random.split(jax.random.key(seed), 9)
    return {
        "electric": gaussian(splits[0], (3, NX, NY, NZ), 1.0, 6.0, ((1, 4), (2, 2), (3, 4)), jnp.float32),
        "material": place_ends(jax.random.randint(splits[1], (NX, NY, NZ), 0, MATS), jax.random.fold_in(splits[1], 1), 0, MATS - 1).astype(jnp.int32),
        "coef_keep": jnp.clip(jax.random.uniform(splits[2], (3, MATS), jnp.float32, 0.6, 1.0), 0.6, 1.0),
        "coef_curl": jnp.clip(jax.random.uniform(splits[3], (3, MATS), jnp.float32, 0.1, 0.5), 0.1, 0.5),
        "huygens_count": draw_huygens_count(jax.random.fold_in(splits[8], 71), 0),
        "huygens_cells": place_ends(jax.random.randint(splits[5], (BRX, BRY, BRZ, HMAX), 0, CX * CY * CZ), jax.random.fold_in(splits[5], 1), 0, (CX * CY * CZ) - 1).astype(jnp.int32),
        "band_tiles": draw_band_tiles(jax.random.fold_in(splits[8], 71), 0),
        "radiation": gaussian(splits[7], (NDB, GROUPS, NBAND, 6, DB, RT), KFAN ** -0.5, 0.0390625, ((0, 4), (1, 8))),
    }


courant = 0.5


def forward_curl(padded):
    anchor = padded[:, :-1, :-1, :-1]
    plus_x = padded[:, 1:, :-1, :-1]
    plus_y = padded[:, :-1, 1:, :-1]
    plus_z = padded[:, :-1, :-1, 1:]
    curl_x = (plus_y[2] - anchor[2]) - (plus_z[1] - anchor[1])
    curl_y = (plus_z[0] - anchor[0]) - (plus_x[2] - anchor[2])
    curl_z = (plus_x[1] - anchor[1]) - (plus_y[0] - anchor[0])
    return jnp.stack([curl_x, curl_y, curl_z])


def backward_curl(padded):
    centre = padded[:, 1:, 1:, 1:]
    minus_x = padded[:, :-1, 1:, 1:]
    minus_y = padded[:, 1:, :-1, 1:]
    minus_z = padded[:, 1:, 1:, :-1]
    curl_x = (centre[2] - minus_y[2]) - (centre[1] - minus_z[1])
    curl_y = (centre[0] - minus_z[0]) - (centre[2] - minus_x[2])
    curl_z = (centre[1] - minus_x[1]) - (centre[0] - minus_y[0])
    return jnp.stack([curl_x, curl_y, curl_z])


def reference(electric, material, coef_keep, coef_curl, huygens_count, huygens_cells, band_tiles, radiation):
    keep = coef_keep[:, material]
    gain = coef_curl[:, material]
    efield = electric
    hfield = jnp.zeros_like(electric)
    cell_x = huygens_cells // (CY * CZ)
    cell_y = (huygens_cells // CZ) % CY
    cell_z = huygens_cells % CZ
    glob_x = jnp.arange(BRX, dtype=jnp.int32)[:, None, None, None] * CX + cell_x
    glob_y = jnp.arange(BRY, dtype=jnp.int32)[None, :, None, None] * CY + cell_y
    glob_z = jnp.arange(BRZ, dtype=jnp.int32)[None, None, :, None] * CZ + cell_z
    active = jnp.arange(HMAX, dtype=jnp.int32)[None, None, None, :] < huygens_count[..., None]
    row_list = []
    for instant in range(STEPS):
        hfield = hfield - courant * forward_curl(jnp.pad(efield, ((0, 0), (0, 1), (0, 1), (0, 1))))
        efield = keep * efield + gain * backward_curl(jnp.pad(hfield, ((0, 0), (1, 0), (1, 0), (1, 0))))
        fields = jnp.concatenate([efield[:, glob_x, glob_y, glob_z], hfield[:, glob_x, glob_y, glob_z]], axis=0)
        row_list.append(jnp.where(active[None], fields, 0.0).astype(jnp.bfloat16))
    values = jnp.stack(row_list, axis=1).reshape(6, STEPS, GROUPS, BRZ * TPB, RT)
    group_ids = jnp.arange(GROUPS, dtype=jnp.int32)[:, None]

    def one_block(operands):
        kernel_block, band_block = operands
        chosen = values[:, :, group_ids, band_block, :]
        return jnp.einsum("csgnr,gncdr->sd", chosen.astype(jnp.float32), kernel_block.astype(jnp.float32))

    blocks = lax.map(one_block, (radiation, jnp.transpose(band_tiles, (1, 0, 2))))
    pattern = jnp.transpose(blocks, (1, 0, 2)).reshape(STEPS, NDIR)
    return efield, hfield, pattern
```

```python
import functools

import jax
import jax.numpy as jnp
from jax import lax
from jax.experimental import pallas as pl
from jax.experimental.pallas import tpu as pltpu
from jax.sharding import PartitionSpec as P

STEPS = 4
COURANT = 0.5
MESH = pl.DeviceIdType.MESH

XLO_Y, XLO_Z = 0, 1
XHI_X, XHI_Y, XHI_Z = 2, 3, 4
YLO_Z, YLO_X = 5, 7
YHI_X, YHI_Y, YHI_Z = 9, 11, 13
ZLO_X, ZLO_Y = 15, 16
ZHI_X, ZHI_Y, ZHI_Z = 17, 18, 19
FACES = 20
EDGE_XZ, EDGE_XY, EDGE_YZ, EDGE_YX, EDGE_ZY, EDGE_ZX = 20, 21, 22, 24, 25, 26
GHOSTS = 27

MESSAGES = (
    (ZLO_X, 1, EDGE_XZ, (1, 0, -1)),
    (XHI_X, 1, EDGE_XY, (1, -1, 0)),
    (YHI_Y, 2, EDGE_YZ, (0, 1, -1)),
    (XLO_Y, 1, EDGE_YX, (-1, 1, 0)),
    (ZHI_Z, 1, EDGE_ZY, (0, -1, 1)),
    (ZHI_Z, 1, EDGE_ZX, (-1, 0, 1)),
    (YHI_X, 6, YHI_X, (0, 1, 0)),
    (YLO_Z, 4, YLO_Z, (0, -1, 0)),
    (ZLO_X, 2, ZLO_X, (0, 0, -1)),
    (ZHI_X, 3, ZHI_X, (0, 0, 1)),
    (XLO_Y, 2, XLO_Y, (-1, 0, 0)),
    (XHI_X, 3, XHI_X, (1, 0, 0)),
)


def kernel(
    sizes,
    electric_in, material_in, keep_in, curl_in, count_in, cells_in, band_in, radiation,
    e_end, h_end, p_end,
    e_out, h_out, pattern, material, coef_keep, coef_curl, count, cells, band, face, ghost, hgx, hgy, hgz, keep, gain, table, zhot, rhot, rows, weights, shares,
    send_sem, recv_sem, row_send, row_recv, share_send, share_recv, load_sem, store_sem,
):
    n_gx, n_gy, n_af = sizes
    groups = n_gx * n_gy
    gx, gy, af = lax.axis_index("gx"), lax.axis_index("gy"), lax.axis_index("af")
    me = (gx, gy, af)
    group = gx * n_gy + gy
    cx, cy, cz = e_out.shape[1:]
    hmax = cells.shape[-1]
    row_tile = radiation.shape[-1]
    tiles = hmax // row_tile
    owned, entries, comps = radiation.shape[0], radiation.shape[2], radiation.shape[3]

    def exists(step):
        ok = None
        for at, d, n in zip(me, step, sizes):
            if d:
                term = (at + d >= 0) if d < 0 else (at + d < n)
                ok = term if ok is None else jnp.logical_and(ok, term)
        return ok

    def place(step):
        return tuple(jnp.clip(at + d, 0, n - 1) if d else at for at, d, n in zip(me, step, sizes))

    def back(step):
        return tuple(-d for d in step)

    def af_peer(off):
        return (gx, gy, lax.rem(af + off, n_af))

    def group_peer(off):
        other = lax.rem(group + off, groups)
        return (other // n_gy, lax.rem(other, n_gy), af)

    def over_groups(body):
        if groups <= 16:
            for off in range(1, groups):
                body(off)
        else:
            def step(off, carry):
                body(off)
                return carry
            lax.fori_loop(1, groups, step, 0)

    loads = [
        pltpu.make_async_copy(src, dst, load_sem.at[i])
        for i, (src, dst) in enumerate((
            (electric_in, e_out), (material_in, material), (keep_in, coef_keep),
            (curl_in, coef_curl), (cells_in, cells), (count_in, count), (band_in, band),
            (radiation, weights),
        ))
    ]
    for load in loads:
        load.start()
    stores = [
        pltpu.make_async_copy(src, dst, store_sem.at[i])
        for i, (src, dst) in enumerate(((e_out, e_end), (h_out, h_end), (pattern, p_end)))
    ]

    barrier = pltpu.get_barrier_semaphore()
    for off in range(1, n_af):
        pl.semaphore_signal(barrier, inc=1, device_id=af_peer(off), device_id_type=MESH)
    over_groups(lambda off: pl.semaphore_signal(
        barrier, inc=1, device_id=group_peer(off), device_id_type=MESH))
    expected = jnp.int32(n_af - 1 + groups - 1)
    for _, _, _, step in MESSAGES:
        if step[2] and (step[0] or step[1]):
            there = exists(step)
            expected = expected + there.astype(jnp.int32)

            @pl.when(there)
            def _(step=step):
                pl.semaphore_signal(barrier, inc=1, device_id=place(step), device_id_type=MESH)

    lane = lax.broadcasted_iota(jnp.int32, (cy, cz), 1)
    sub = lax.broadcasted_iota(jnp.int32, (cy, cz), 0)
    lane2 = lax.broadcasted_iota(jnp.int32, (cx, cz), 1)
    sub2 = lax.broadcasted_iota(jnp.int32, (cx, cz), 0)

    def up_z(v, col):
        n = v.shape[0]
        return jnp.where((lane if n == cy else lane2) == cz - 1, col, pltpu.roll(v, cz - 1, 1))

    def up_s(v, row):
        n = v.shape[0]
        return jnp.where((sub if n == cy else sub2) == n - 1, row, pltpu.roll(v, n - 1, 0))

    def pack_plane(t, i, ex, ey, ez, packed):
        face[t, YLO_Z + i // 8, i % 8 : i % 8 + 1, :] = ez[0:1]
        face[t, YLO_X + i // 8, i % 8 : i % 8 + 1, :] = ex[0:1]
        face[t, YHI_X + i // 8, i % 8 : i % 8 + 1, :] = ex[cy - 1 : cy]
        face[t, YHI_Y + i // 8, i % 8 : i % 8 + 1, :] = ey[cy - 1 : cy]
        face[t, YHI_Z + i // 8, i % 8 : i % 8 + 1, :] = ez[cy - 1 : cy]
        if i == 0:
            face[t, XLO_Y] = ey
            face[t, XLO_Z] = ez
        if i == cx - 1:
            face[t, XHI_X] = ex
            face[t, XHI_Y] = ey
            face[t, XHI_Z] = ez
        cols = (ex[:, 0:1], ey[:, 0:1], ex[:, cz - 1 :], ey[:, cz - 1 :], ez[:, cz - 1 :])
        packed = [jnp.where(lane == i, col, p) for col, p in zip(cols, packed)]
        if i == cx - 1:
            for slot, p in zip((ZLO_X, ZLO_Y, ZHI_X, ZHI_Y, ZHI_Z), packed):
                face[t, slot] = p
        return packed

    loads[0].wait()
    nothing = [jnp.zeros((cy, cz), jnp.float32)] * 5
    packed = nothing
    for i in range(cx):
        packed = pack_plane(0, i, e_out[0, i], e_out[1, i], e_out[2, i], packed)

    for m, (_, n, at, step) in enumerate(MESSAGES):
        @pl.when(jnp.logical_not(exists(back(step))))
        def _(n=n, at=at):
            for t in range(STEPS):
                for r in range(at, at + n):
                    ghost[t, r] = jnp.zeros((cy, cz), jnp.float32)

    def message(t, m):
        first, n, at, step = MESSAGES[m]
        return pltpu.make_async_remote_copy(
            src_ref=face.at[t, pl.ds(first, n)],
            dst_ref=ghost.at[t, pl.ds(at, n)],
            send_sem=send_sem.at[t, m],
            recv_sem=recv_sem.at[t, m],
            device_id=place(step),
            device_id_type=MESH,
        )

    def send_faces(t):
        for m in range(len(MESSAGES)):
            @pl.when(exists(MESSAGES[m][3]))
            def _(m=m):
                message(t, m).start()

    def receive_faces(t):
        for m in range(len(MESSAGES)):
            @pl.when(exists(back(MESSAGES[m][3])))
            def _(m=m):
                message(t, m).wait_recv()

    pl.semaphore_wait(barrier, expected)
    send_faces(0)

    for load in loads[1:-1]:
        load.wait()
    table[...] = jnp.zeros_like(table)
    mats = coef_keep.shape[1]
    table[0:3, 0:mats] = coef_keep[...]
    table[3:6, 0:mats] = coef_curl[...]
    for c in range(6):
        row = jnp.broadcast_to(table[c : c + 1, :], (cy, cz))
        for i in range(cx):
            picked = jnp.take_along_axis(row, material[i], axis=1, mode="promise_in_bounds")
            if c < 3:
                keep[c, i] = picked
            else:
                gain[c - 3, i] = picked
    cell = jnp.broadcast_to(cells[...].reshape(1, hmax), (cz, hmax))
    zhot[...] = (lax.broadcasted_iota(jnp.int32, (cz, hmax), 0) == lax.rem(cell, cz)).astype(
        jnp.float32).astype(jnp.bfloat16)
    cell = jnp.broadcast_to(cells[...].reshape(1, hmax), (cx * cy, hmax))
    live = lax.broadcasted_iota(jnp.int32, (cx * cy, hmax), 1) < count[0, 0, 0]
    rhot[...] = jnp.logical_and(
        lax.broadcasted_iota(jnp.int32, (cx * cy, hmax), 0) == lax.div(cell, cz), live
    ).astype(jnp.float32)

    has_x = (gx > 0).astype(jnp.float32)
    has_y = (gy > 0).astype(jnp.float32)
    has_z = (af > 0).astype(jnp.float32)

    def row_message(t, off):
        mine = rows.at[t, pl.ds(af * (tiles // 2), tiles // 2)]
        return pltpu.make_async_remote_copy(
            src_ref=mine, dst_ref=mine,
            send_sem=row_send.at[t, off], recv_sem=row_recv.at[t, off],
            device_id=af_peer(off), device_id_type=MESH,
        )

    for t in range(STEPS):
        receive_faces(t)

        def two(r):
            return ghost[t, r : r + 2].reshape(cx, cz)

        def grown(old, ref, at, change, there):
            new = -COURANT * change * there
            if t:
                new = old + new
            ref[at] = new

        ex, ey, ez = ghost[t, XHI_X], ghost[t, XHI_Y], ghost[t, XHI_Z]
        dz_ex = up_z(ex, ghost[t, EDGE_XZ][:, cx - 1 : cx]) - ex
        dy_ex = up_s(ex, ghost[t, EDGE_XY, 0:1, :]) - ex
        grown(hgx[0], hgx, 0, dz_ex - (e_out[2, 0] - ez), has_x)
        grown(hgx[1], hgx, 1, (e_out[1, 0] - ey) - dy_ex, has_x)

        ex, ey, ez = two(YHI_X), two(YHI_Y), two(YHI_Z)
        low_z = face[t, YLO_Z : YLO_Z + 2].reshape(cx, cz)
        low_x = face[t, YLO_X : YLO_X + 2].reshape(cx, cz)
        dz_ey = up_z(ey, two(EDGE_YZ)[:, 0:1]) - ey
        dx_ey = up_s(ey, ghost[t, EDGE_YX, cy - 1 : cy, :]) - ey
        grown(hgy[0], hgy, 0, (low_z - ez) - dz_ey, has_y)
        grown(hgy[1], hgy, 1, dx_ey - (low_x - ex), has_y)

        ex, ey, ez = ghost[t, ZHI_X], ghost[t, ZHI_Y], ghost[t, ZHI_Z]
        dy_ez = up_s(ez, ghost[t, EDGE_ZY, 0:1, :]) - ez
        dx_ez = jnp.where(
            lane == cx - 1, ghost[t, EDGE_ZX][:, 0:1], pltpu.roll(ez, cz - 1, 1)) - ez
        grown(hgz[0], hgz, 0, dy_ez - (face[t, ZLO_Y] - ey), has_z)
        grown(hgz[1], hgz, 1, (face[t, ZLO_X] - ex) - dx_ez, has_z)

        top_x, top_y = ghost[t, ZLO_X], ghost[t, ZLO_Y]
        low_hx, low_hy = hgz[0], hgz[1]
        hy_last, hz_last = hgx[0], hgx[1]
        packed = nothing
        ex, ey, ez = e_out[0, 0], e_out[1, 0], e_out[2, 0]
        for i in range(cx):
            if i + 1 < cx:
                exn, eyn, ezn = e_out[0, i + 1], e_out[1, i + 1], e_out[2, i + 1]
            else:
                exn, eyn, ezn = None, ghost[t, XLO_Y], ghost[t, XLO_Z]
            up = (i // 8, slice(i % 8, i % 8 + 1))
            ez_y = up_s(ez, ghost[t, YLO_Z + up[0], up[1], :])
            ex_y = up_s(ex, ghost[t, YLO_X + up[0], up[1], :])
            ex_z = up_z(ex, top_x[:, i : i + 1])
            ey_z = up_z(ey, top_y[:, i : i + 1])
            hx = -COURANT * ((ez_y - ez) - (ey_z - ey))
            hy = -COURANT * ((ex_z - ex) - (ezn - ez))
            hz = -COURANT * ((eyn - ey) - (ex_y - ex))
            if t:
                hx = h_out[0, i] + hx
                hy = h_out[1, i] + hy
                hz = h_out[2, i] + hz
            h_out[0, i], h_out[1, i], h_out[2, i] = hx, hy, hz
            hx_y = jnp.where(sub == 0, hgy[0, i : i + 1, :], pltpu.roll(hx, 1, 0))
            hz_y = jnp.where(sub == 0, hgy[1, i : i + 1, :], pltpu.roll(hz, 1, 0))
            hx_z = jnp.where(lane == 0, low_hx[:, i : i + 1], pltpu.roll(hx, 1, 1))
            hy_z = jnp.where(lane == 0, low_hy[:, i : i + 1], pltpu.roll(hy, 1, 1))
            curl_x = (hz - hz_y) - (hy - hy_z)
            curl_y = (hx - hx_z) - (hz - hz_last)
            curl_z = (hy - hy_last) - (hx - hx_y)
            hy_last, hz_last = hy, hz
            new_x = keep[0, i] * ex + gain[0, i] * curl_x
            new_y = keep[1, i] * ey + gain[1, i] * curl_y
            new_z = keep[2, i] * ez + gain[2, i] * curl_z
            e_out[0, i], e_out[1, i], e_out[2, i] = new_x, new_y, new_z
            if t + 1 < STEPS:
                packed = pack_plane(t + 1, i, new_x, new_y, new_z, packed)
            ex, ey, ez = exn, eyn, ezn
        if t + 1 < STEPS:
            send_faces(t + 1)
        else:
            stores[0].start()
            stores[1].start()

        picked = []
        for k in range(comps):
            field = e_out if k < 3 else h_out
            values = field[k % 3].reshape(cx * cy, cz).astype(jnp.bfloat16)
            column = jnp.dot(values, zhot[...], preferred_element_type=jnp.float32)
            picked.append(jnp.sum(column * rhot[...], axis=0, keepdims=True))
        picked.append(jnp.zeros((8 - comps, hmax), jnp.float32))
        picked = jnp.concatenate(picked, axis=0)
        for q in range(tiles // 2):
            at = 2 * q * row_tile
            pair = [picked[:, at : at + row_tile], picked[:, at + row_tile : at + 2 * row_tile]]
            rows[t, af * (tiles // 2) + q] = jnp.concatenate(pair, axis=0).astype(jnp.bfloat16)
        for off in range(1, n_af):
            row_message(t, off).start()

    loads[-1].wait()
    for t in range(STEPS):
        for off in range(1, n_af):
            row_message(t, off).wait_recv()

    sums = []
    for o in range(owned):
        total = None
        for n in range(entries):
            tile = band[0, o, n]
            pairs = [rows[t, tile // 2].astype(jnp.float32) for t in range(STEPS)]
            odd = lax.rem(tile, 2)
            segment = jnp.concatenate(
                [jnp.where(odd == 1, pair[8:], pair[:8]) for pair in pairs], axis=0)
            term = lax.dot_general(
                segment.astype(jnp.bfloat16),
                weights[o, 0, n].reshape(comps * row_tile, row_tile),
                (((1,), (1,)), ((), ())),
                preferred_element_type=jnp.float32,
            )
            total = term if total is None else total + term
        for t in range(STEPS):
            own = total[t * 8 : t * 8 + 1, 0:row_tile]
            for k in range(1, comps):
                own = own + total[t * 8 + k : t * 8 + k + 1, k * row_tile : (k + 1) * row_tile]
            sums.append(own)
    shares[group] = jnp.concatenate(sums, axis=0)

    def share_message(off):
        return pltpu.make_async_remote_copy(
            src_ref=shares.at[group], dst_ref=shares.at[group],
            send_sem=share_send.at[off], recv_sem=share_recv.at[off],
            device_id=group_peer(off), device_id_type=MESH,
        )

    over_groups(lambda off: share_message(off).start())
    for t in range(STEPS):
        for off in range(1, n_af):
            row_message(t, off).wait_send()
        for m in range(len(MESSAGES)):
            @pl.when(exists(MESSAGES[m][3]))
            def _(t=t, m=m):
                message(t, m).wait_send()
    stores[0].wait()
    stores[1].wait()
    over_groups(lambda off: share_message(off).wait_recv())
    total = jnp.sum(shares[...], axis=0)
    for o in range(owned):
        pattern[:, o * row_tile : (o + 1) * row_tile] = total[o * STEPS : (o + 1) * STEPS]
    stores[2].start()

    over_groups(lambda off: share_message(off).wait_send())
    stores[2].wait()


def finish(e_in, h_in, p_in, e_out, h_out, p_out, sem):
    stores = [
        pltpu.make_async_copy(src, dst, sem.at[i])
        for i, (src, dst) in enumerate(((p_in, p_out), (e_in, e_out), (h_in, h_out)))
    ]
    for store in stores:
        store.start()
    for store in stores:
        store.wait()


def on_device(
    sizes,
    electric, material, coef_keep, coef_curl, huygens_count, huygens_cells, band_tiles, radiation,
):
    cx, cy, cz = electric.shape[1:]
    hmax = huygens_cells.shape[-1]
    owned, row_tile = radiation.shape[0], radiation.shape[-1]
    n_gx, n_gy, n_af = sizes
    groups = n_gx * n_gy
    tiles = n_af * hmax // row_tile
    f32 = jnp.float32
    out_shape = (
        jax.ShapeDtypeStruct(electric.shape, f32),
        jax.ShapeDtypeStruct(electric.shape, f32),
        jax.ShapeDtypeStruct((STEPS, owned * row_tile), f32),
    )
    hbm = pl.BlockSpec(memory_space=pltpu.HBM)
    anyw = pl.BlockSpec(memory_space=pl.ANY)
    operands = [pltpu.with_memory_space_constraint(v, pltpu.HBM) for v in (electric, material, coef_keep, coef_curl)] + [huygens_count] + [
        pltpu.with_memory_space_constraint(v, pltpu.HBM) for v in (huygens_cells, band_tiles, radiation)]
    results = pl.pallas_call(
        functools.partial(kernel, sizes),
        out_shape=out_shape,
        in_specs=[hbm] * 8,
        out_specs=(anyw,) * 3,
        scratch_shapes=[
            pltpu.VMEM(electric.shape, f32),
            pltpu.VMEM(electric.shape, f32),
            pltpu.VMEM((STEPS, owned * row_tile), f32),
            pltpu.VMEM(material.shape, jnp.int32),
            pltpu.VMEM(coef_keep.shape, f32),
            pltpu.VMEM(coef_curl.shape, f32),
            pltpu.SMEM(huygens_count.shape, jnp.int32),
            pltpu.VMEM(huygens_cells.shape, jnp.int32),
            pltpu.SMEM(band_tiles.shape, jnp.int32),
            pltpu.VMEM((STEPS, FACES, cy, cz), f32),
            pltpu.VMEM((STEPS, GHOSTS, cy, cz), f32),
            pltpu.VMEM((2, cy, cz), f32),
            pltpu.VMEM((2, cx, cz), f32),
            pltpu.VMEM((2, cy, cz), f32),
            pltpu.VMEM((3, cx, cy, cz), f32),
            pltpu.VMEM((3, cx, cy, cz), f32),
            pltpu.VMEM((8, cz), f32),
            pltpu.VMEM((cz, hmax), jnp.bfloat16),
            pltpu.VMEM((cx * cy, hmax), f32),
            pltpu.VMEM((STEPS, tiles // 2, 16, row_tile), jnp.bfloat16),
            pltpu.VMEM(radiation.shape, jnp.bfloat16),
            pltpu.VMEM((groups, owned * STEPS, row_tile), f32),
            pltpu.SemaphoreType.DMA((STEPS, len(MESSAGES))),
            pltpu.SemaphoreType.DMA((STEPS, len(MESSAGES))),
            pltpu.SemaphoreType.DMA((STEPS, n_af)),
            pltpu.SemaphoreType.DMA((STEPS, n_af)),
            pltpu.SemaphoreType.DMA((groups,)),
            pltpu.SemaphoreType.DMA((groups,)),
            pltpu.SemaphoreType.DMA((8,)),
            pltpu.SemaphoreType.DMA((3,)),
        ],
        compiler_params=pltpu.CompilerParams(
            collective_id=0, has_side_effects=True, vmem_limit_bytes=16 * 1024 * 1024
        ),
    )(*operands)
    return pl.pallas_call(
        finish,
        out_shape=out_shape,
        in_specs=[anyw] * 3,
        out_specs=(hbm,) * 3,
        scratch_shapes=[pltpu.SemaphoreType.DMA((3,))],
        compiler_params=pltpu.CompilerParams(vmem_limit_bytes=16 * 1024 * 1024),
    )(*results)


def solution(mesh):
    placed = (
        P(None, "gx", "gy", "af"),
        P("gx", "gy", "af"),
        P(),
        P(),
        P("gx", "gy", "af"),
        P("gx", "gy", "af", None),
        P(("gx", "gy"), "af", None),
        P("af", ("gx", "gy"), None, None, None, None),
    )
    sizes = (mesh.shape["gx"], mesh.shape["gy"], mesh.shape["af"])
    return jax.shard_map(
        functools.partial(on_device, sizes),
        mesh=mesh,
        in_specs=placed,
        out_specs=(P(None, "gx", "gy", "af"), P(None, "gx", "gy", "af"), P(None, "af")),
        check_vma=False,
    )
```

```python
import functools
import itertools

import jax
import jax.numpy as jnp
from jax import lax
from jax.experimental import pallas as pl
from jax.experimental.pallas import tpu as pltpu
from jax.sharding import PartitionSpec as P

STEPS = 4
COURANT = 0.5
MESH = pl.DeviceIdType.MESH
f32, bf16 = jnp.float32, jnp.bfloat16

STEPS_TO = sorted(
    (d for d in itertools.product((-1, 0, 1), repeat=3) if any(d)),
    key=lambda d: (abs(d[2]), -abs(d[1]), abs(d[0])),
)


def kernel(
    sizes,
    electric_in, material_in, keep_in, curl_in, count_in, cells_in, band_in, radiation,
    e_end, h_end, p_end,
    e_out, h_out, pattern, material, coef_keep, coef_curl, count, cells, band,
    ef, gf, keep, gain, dz, ahead, behind, spread, low_mask,
    x_pack, y_pack, z_pack, x_ghost, y_ghost, z_ghost,
    table, zhot, rhot, rows, weights, shares,
    send_sem, recv_sem, row_send, row_recv, share_send, share_recv, load_sem, store_sem,
):
    n_gx, n_gy, n_af = sizes
    groups = n_gx * n_gy
    gx, gy, af = lax.axis_index("gx"), lax.axis_index("gy"), lax.axis_index("af")
    me = (gx, gy, af)
    group = gx * n_gy + gy
    cx, cy, cz = e_out.shape[1:]
    hmax = cells.shape[-1]
    row_tile = radiation.shape[-1]
    tiles = hmax // row_tile
    owned, entries, comps = radiation.shape[0], radiation.shape[2], radiation.shape[3]

    def exists(step):
        ok = None
        for at, d, n in zip(me, step, sizes):
            if d:
                term = (at + d >= 0) if d < 0 else (at + d < n)
                ok = term if ok is None else jnp.logical_and(ok, term)
        return ok

    def place(step):
        return tuple(jnp.clip(at + d, 0, n - 1) if d else at for at, d, n in zip(me, step, sizes))

    def back(step):
        return tuple(-d for d in step)

    def af_peer(off):
        return (gx, gy, lax.rem(af + off, n_af))

    def group_peer(off):
        other = lax.rem(group + off, groups)
        return (other // n_gy, lax.rem(other, n_gy), af)

    def over_groups(body):
        if groups <= 16:
            for off in range(1, groups):
                body(off)
        else:
            def step(off, carry):
                body(off)
                return carry
            lax.fori_loop(1, groups, step, 0)

    halo = STEPS
    planes = cx + 2 * halo
    own = pl.ds(halo, cx)
    wide = 2 * cz
    loads = [
        pltpu.make_async_copy(src, dst, load_sem.at[i])
        for i, (src, dst) in enumerate((
            (electric_in, ef.at[:, own, 0, :, pl.ds(0, cz)]), (material_in, material),
            (keep_in, coef_keep), (curl_in, coef_curl), (cells_in, cells), (count_in, count),
            (band_in, band), (radiation, weights),
        ))
    ]
    for load in loads:
        load.start()
    stores = [
        pltpu.make_async_copy(src, dst, store_sem.at[i])
        for i, (src, dst) in enumerate(((e_out, e_end), (h_out, h_end), (pattern, p_end)))
    ]

    barrier = pltpu.get_barrier_semaphore()
    for off in range(1, n_af):
        pl.semaphore_signal(barrier, inc=1, device_id=af_peer(off), device_id_type=MESH)
    over_groups(lambda off: pl.semaphore_signal(
        barrier, inc=1, device_id=group_peer(off), device_id_type=MESH))
    expected = jnp.int32(n_af - 1 + groups - 1)
    for step in STEPS_TO:
        if step[2] and (step[0] or step[1]):
            there = exists(step)
            expected = expected + there.astype(jnp.int32)

            @pl.when(there)
            def _(step=step):
                pl.semaphore_signal(barrier, inc=1, device_id=place(step), device_id_type=MESH)

    lane = lax.broadcasted_iota(jnp.int32, (cy, cz), 1)
    sub = lax.broadcasted_iota(jnp.int32, (cy, cz), 0)
    low_rows = sub < halo
    edge = 2 * halo

    at = lax.broadcasted_iota(jnp.int32, (cz, cz), 0)
    to = lax.broadcasted_iota(jnp.int32, (cz, cz), 1)
    packed_at = jnp.where(to < halo, to, jnp.where(to >= cz - halo, to - (cz - edge), -cx * cz))
    for i in range(cx):
        spread[:, i * cz : (i + 1) * cz] = (at == packed_at + i * edge).astype(f32).astype(bf16)

    loads[0].wait()
    loads[1].wait()

    def own_plane(c, i):
        if c < 3:
            return ef[c, halo + i, 0, :, 0:cz]
        return material[i].astype(f32)

    for c in range(4):
        for side, first in ((0, 0), (1, cx - halo)):
            for j in range(halo // 2):
                pair = [own_plane(c, first + 2 * j), own_plane(c, first + 2 * j + 1)]
                x_pack[side, c, j] = jnp.concatenate(pair, axis=0).astype(bf16)
        for j in range(cx // 4):
            four = [own_plane(c, 4 * j + r) for r in range(4)]
            turned = [pltpu.roll(four[1], halo, 0), pltpu.roll(four[3], halo, 0)]
            low = [jnp.where(low_rows, four[2 * r], turned[r]) for r in range(2)]
            high = [jnp.where(low_rows, turned[r], four[2 * r]) for r in range(2)]
            y_pack[0, c, j] = jnp.concatenate(low, axis=0).astype(bf16)
            y_pack[1, c, j] = jnp.concatenate(high, axis=0).astype(bf16)
    lines = [jnp.concatenate([own_plane(c, i) for i in range(cx)], axis=1) for c in range(4)]
    ends = lax.dot_general(
        jnp.concatenate(lines, axis=0).astype(bf16), spread[...],
        (((1,), (1,)), ((), ())), preferred_element_type=f32)
    z_pack[...] = ends.reshape(2, 2 * cy, cz).astype(bf16)

    def message(step):
        dx, dy, dz_ = step
        m = STEPS_TO.index(step)
        if dz_:
            src = z_pack
            dst = z_ghost.at[0 if dz_ < 0 else 1, (0, 2, 1)[dy], (0, 2, 1)[dx]]
        elif dy:
            side = 0 if dy < 0 else 1
            n = 1 if dx else cx // 4
            first = cx // 4 - 1 if dx > 0 else 0
            to = (1, 0, cx // 4 + 1)[dx]
            src = y_pack.at[side, :, pl.ds(first, n)]
            dst = y_ghost.at[side, :, pl.ds(to, n)]
        else:
            src = x_pack.at[1 if dx > 0 else 0]
            dst = x_ghost.at[0 if dx > 0 else 1]
        return pltpu.make_async_remote_copy(
            src_ref=src, dst_ref=dst, send_sem=send_sem.at[m], recv_sem=recv_sem.at[m],
            device_id=place(step), device_id_type=MESH,
        )

    pl.semaphore_wait(barrier, expected)
    for step in STEPS_TO:
        @pl.when(exists(step))
        def _(step=step):
            message(step).start()

    outside = float(coef_keep.shape[1])
    pair_row = lax.broadcasted_iota(jnp.int32, (2 * cy, cz), 0)
    for step in STEPS_TO:
        @pl.when(jnp.logical_not(exists(back(step))))
        def _(step=step):
            dx, dy, dz_ = step
            nothing = jnp.zeros((2 * cy, cz), bf16)
            beyond = jnp.full((2 * cy, cz), outside, bf16)
            if dz_:
                place_of = (0 if dz_ < 0 else 1, (0, 2, 1)[dy], (0, 2, 1)[dx])
                z_ghost[place_of + (0,)] = nothing
                z_ghost[place_of + (1,)] = jnp.where(
                    pair_row >= cy, outside, 0.0).astype(bf16)
            elif dy:
                n = 1 if dx else cx // 4
                to = (1, 0, cx // 4 + 1)[dx]
                for c in range(4):
                    for j in range(to, to + n):
                        y_ghost[0 if dy < 0 else 1, c, j] = nothing if c < 3 else beyond
            else:
                for c in range(4):
                    for j in range(halo // 2):
                        x_ghost[0 if dx > 0 else 1, c, j] = nothing if c < 3 else beyond

    for load in loads[2:-1]:
        load.wait()
    table[...] = jnp.zeros_like(table)
    mats = coef_keep.shape[1]
    table[0:3, 0:mats] = coef_keep[...]
    table[3:6, 0:mats] = -COURANT * coef_curl[...]
    factors = [jnp.broadcast_to(table[c : c + 1, :], (cy, cz)) for c in range(6)]

    def picked_factors(classes):
        return [
            jnp.take_along_axis(row, classes, axis=1, mode="promise_in_bounds") for row in factors
        ]

    def set_factors(p, t, classes):
        for c, value in enumerate(picked_factors(classes)):
            (keep if c < 3 else gain)[c % 3, p, t, :, 0:cz] = value

    for i in range(cx):
        set_factors(halo + i, 0, material[i])
    row_at = lax.broadcasted_iota(jnp.int32, (wide, wide), 0)
    col_at = lax.broadcasted_iota(jnp.int32, (wide, wide), 1)
    same = (row_at == col_at).astype(f32)
    ahead[...] = ((row_at == lax.rem(col_at + 1, wide)).astype(f32) - same).astype(bf16)
    behind[...] = (same - (lax.rem(row_at + 1, wide) == col_at).astype(f32)).astype(bf16)
    cell = jnp.broadcast_to(cells[...].reshape(1, hmax), (cz, hmax))
    zhot[...] = (lax.broadcasted_iota(jnp.int32, (cz, hmax), 0) == lax.rem(cell, cz)).astype(
        f32).astype(bf16)
    cell = jnp.broadcast_to(cells[...].reshape(1, hmax), (cx * cy, hmax))
    live = lax.broadcasted_iota(jnp.int32, (cx * cy, hmax), 1) < count[0, 0, 0]
    rhot[...] = jnp.logical_and(
        lax.broadcasted_iota(jnp.int32, (cx * cy, hmax), 0) == lax.div(cell, cz), live
    ).astype(f32)
    has_x = (gx > 0).astype(f32)
    has_y = (gy > 0).astype(f32)
    has_z = (af > 0).astype(f32)
    wide_lane = lax.broadcasted_iota(jnp.int32, (cy, wide), 1)
    wide_sub = lax.broadcasted_iota(jnp.int32, (cy, wide), 0)
    for x in range(2):
        for t in range(2):
            mask = jnp.where(wide_lane >= cz + cz // 2, has_z, 1.0)
            if t:
                mask = mask * jnp.where(wide_sub >= halo, has_y, 1.0)
            low_mask[2 * x + t] = mask * has_x if x else mask

    for step in STEPS_TO:
        @pl.when(exists(back(step)))
        def _(step=step):
            message(step).wait_recv()

    def as_classes(v):
        return v.astype(jnp.int32)

    for side, first in ((0, 0), (1, cx + halo)):
        for j in range(halo // 2):
            for c in range(4):
                pair = x_ghost[side, c, j].astype(f32)
                for r in range(2):
                    p = first + 2 * j + r
                    v = pair[r * cy : (r + 1) * cy]
                    if c < 3:
                        ef[c, p, 0, :, 0:cz] = v
                    else:
                        set_factors(p, 0, as_classes(v))
    for j in range(planes // 4):
        for c in range(4):
            above = y_ghost[0, c, j].astype(f32)
            below = y_ghost[1, c, j].astype(f32)
            for r in range(2):
                up, down = above[r * cy : (r + 1) * cy], below[r * cy : (r + 1) * cy]
                both = (
                    jnp.where(low_rows, up, down),
                    pltpu.roll(jnp.where(low_rows, down, up), halo, 0),
                )
                for q in range(2):
                    p = 4 * j + 2 * r + q
                    if c < 3:
                        ef[c, p, 1, :, 0:cz] = both[q]
                    else:
                        set_factors(p, 1, as_classes(both[q]))
    from_above = lax.rem(lane, edge) < halo

    def ends_of(c, t, chunk):
        def joined(dyi, dxi):
            at = (slice((c % 2) * cy, (c % 2 + 1) * cy), slice(None))
            return jnp.where(
                from_above, z_ghost[0, dyi, dxi, c // 2][at].astype(f32),
                z_ghost[1, dyi, dxi, c // 2][at].astype(f32))

        def over_x(dyi):
            if chunk == 0:
                return joined(dyi, 0)
            return jnp.where(lane < cz // 2, joined(dyi, 1), joined(dyi, 2))

        return over_x(0) if t == 0 else jnp.where(low_rows, over_x(1), over_x(2))

    for chunk in range(2):
        if chunk == 0:
            blocks = [(0, [halo + i for i in range(cx)])]
        else:
            blocks = [(0, [cx + halo + i for i in range(halo)]), (cx - halo, list(range(halo)))]
        field = jnp.concatenate(
            [ends_of(c, t, chunk) for c in range(3) for t in range(2)], axis=0).astype(bf16)
        found = [picked_factors(as_classes(ends_of(3, t, chunk))) for t in range(2)]
        factor = jnp.concatenate([found[t][c] for c in range(6) for t in range(2)], axis=0)
        rough = factor.astype(bf16)
        rest = (factor - rough.astype(f32)).astype(bf16)
        for first, where_to in blocks:
            part = spread[:, first * cz : (first + len(where_to)) * cz]
            a = jnp.dot(field, part, preferred_element_type=f32)
            b = jnp.dot(rough, part, preferred_element_type=f32)
            b = b + jnp.dot(rest, part, preferred_element_type=f32)
            for i, p in enumerate(where_to):
                cols = slice(i * cz, (i + 1) * cz)
                for t in range(2):
                    for c in range(3):
                        at_row = (2 * c + t) * cy
                        ef[c, p, t, :, cz:wide] = a[at_row : at_row + cy, cols]
                        keep[c, p, t, :, cz:wide] = b[at_row : at_row + cy, cols]
                        at_row += 6 * cy
                        gain[c, p, t, :, cz:wide] = b[at_row : at_row + cy, cols]

    def row_message(t, off):
        mine = rows.at[t, pl.ds(af * (tiles // 2), tiles // 2)]
        return pltpu.make_async_remote_copy(
            src_ref=mine, dst_ref=mine,
            send_sem=row_send.at[t, off], recv_sem=row_recv.at[t, off],
            device_id=af_peer(off), device_id_type=MESH,
        )

    def up_y(v):
        r = [pltpu.roll(tile, cy - 1, 0) for tile in v]
        last = wide_sub == cy - 1
        return [jnp.where(last, r[1], r[0]), jnp.where(last, r[0], r[1])]

    def down_y(v):
        r = [pltpu.roll(tile, 1, 0) for tile in v]
        first = wide_sub == 0
        return [jnp.where(first, r[1], r[0]), jnp.where(first, r[0], r[1])]

    def along_z(ref, c, first, n, matrix, width):
        v = ref[c, first : first + n].reshape(n * 2 * cy, wide)
        rough = v.astype(bf16)
        rest = (v - rough.astype(f32)).astype(bf16)
        change = jnp.dot(rough, matrix[:, 0:width], preferred_element_type=f32)
        change = change + jnp.dot(rest, matrix[:, 0:width], preferred_element_type=f32)
        dz[c, first : first + n, :, :, 0:width] = change.reshape(n, 2, cy, width)

    for t in range(STEPS):
        first, last = t, planes - 2 - t
        for c in range(2):
            along_z(ef, c, first, last - first + 1, ahead, wide)
        for p in range(first, last + 1):
            ex, ey, ez = [[ef[c, p, y] for y in range(2)] for c in range(3)]
            ez_y, ex_y = up_y(ez), up_y(ex)
            for y in range(2):
                change = (
                    (ez_y[y] - ez[y]) - dz[1, p, y],
                    dz[0, p, y] - (ef[2, p + 1, y] - ez[y]),
                    (ef[1, p + 1, y] - ey[y]) - (ex_y[y] - ex[y]),
                )
                mask = low_mask[(2 if p < halo else 0) + y]
                for c in range(3):
                    new = change[c] * mask
                    if t:
                        new = gf[c, p, y] + new
                    gf[c, p, y] = new
        first = t + 1
        end = t + 1 == STEPS
        width = cz if end else wide
        for c in range(2):
            along_z(gf, c, first, last - first + 1, behind, width)
        for p in range(first, last + 1):
            hx, hz = [[gf[c, p, y] for y in range(2)] for c in (0, 2)]
            hx_y, hz_y = down_y(hx), down_y(hz)
            for y in range(1 if end else 2):
                w = slice(0, width)
                change = (
                    (hz[y] - hz_y[y])[:, w] - dz[1, p, y, :, w],
                    dz[0, p, y, :, w] - (hz[y] - gf[2, p - 1, y])[:, w],
                    (gf[1, p, y] - gf[1, p - 1, y])[:, w] - (hx[y] - hx_y[y])[:, w],
                )
                for c in range(3):
                    new = keep[c, p, y, :, w] * ef[c, p, y, :, w] + gain[c, p, y, :, w] * change[c]
                    if end:
                        e_out[c, p - halo] = new
                        h_out[c, p - halo] = -COURANT * gf[c, p, 0, :, w]
                    else:
                        ef[c, p, y] = new
        if end:
            stores[0].start()
            stores[1].start()

        picked = []
        for k in range(comps):
            if end:
                field = (e_out if k < 3 else h_out)[k % 3]
            else:
                field = (ef if k < 3 else gf)[k % 3, halo : halo + cx, 0, :, 0:cz]
            values = field.reshape(cx * cy, cz)
            if k >= 3 and not end:
                values = -COURANT * values
            column = jnp.dot(values.astype(bf16), zhot[...], preferred_element_type=f32)
            picked.append(jnp.sum(column * rhot[...], axis=0, keepdims=True))
        picked.append(jnp.zeros((8 - comps, hmax), jnp.float32))
        picked = jnp.concatenate(picked, axis=0)
        for q in range(tiles // 2):
            at = 2 * q * row_tile
            pair = [picked[:, at : at + row_tile], picked[:, at + row_tile : at + 2 * row_tile]]
            rows[t, af * (tiles // 2) + q] = jnp.concatenate(pair, axis=0).astype(jnp.bfloat16)
        for off in range(1, n_af):
            row_message(t, off).start()

    loads[-1].wait()
    for t in range(STEPS):
        for off in range(1, n_af):
            row_message(t, off).wait_recv()

    sums = []
    for o in range(owned):
        total = None
        for n in range(entries):
            tile = band[0, o, n]
            pairs = [rows[t, tile // 2].astype(jnp.float32) for t in range(STEPS)]
            odd = lax.rem(tile, 2)
            segment = jnp.concatenate(
                [jnp.where(odd == 1, pair[8:], pair[:8]) for pair in pairs], axis=0)
            term = lax.dot_general(
                segment.astype(jnp.bfloat16),
                weights[o, 0, n].reshape(comps * row_tile, row_tile),
                (((1,), (1,)), ((), ())),
                preferred_element_type=jnp.float32,
            )
            total = term if total is None else total + term
        for t in range(STEPS):
            own = total[t * 8 : t * 8 + 1, 0:row_tile]
            for k in range(1, comps):
                own = own + total[t * 8 + k : t * 8 + k + 1, k * row_tile : (k + 1) * row_tile]
            sums.append(own)
    shares[group] = jnp.concatenate(sums, axis=0)

    def share_message(off):
        return pltpu.make_async_remote_copy(
            src_ref=shares.at[group], dst_ref=shares.at[group],
            send_sem=share_send.at[off], recv_sem=share_recv.at[off],
            device_id=group_peer(off), device_id_type=MESH,
        )

    over_groups(lambda off: share_message(off).start())
    for t in range(STEPS):
        for off in range(1, n_af):
            row_message(t, off).wait_send()
    for step in STEPS_TO:
        @pl.when(exists(step))
        def _(step=step):
            message(step).wait_send()
    stores[0].wait()
    stores[1].wait()
    over_groups(lambda off: share_message(off).wait_recv())
    total = jnp.sum(shares[...], axis=0)
    for o in range(owned):
        pattern[:, o * row_tile : (o + 1) * row_tile] = total[o * STEPS : (o + 1) * STEPS]
    stores[2].start()

    over_groups(lambda off: share_message(off).wait_send())
    stores[2].wait()


def finish(e_in, h_in, p_in, e_out, h_out, p_out, sem):
    stores = [
        pltpu.make_async_copy(src, dst, sem.at[i])
        for i, (src, dst) in enumerate(((p_in, p_out), (e_in, e_out), (h_in, h_out)))
    ]
    for store in stores:
        store.start()
    for store in stores:
        store.wait()


def on_device(
    sizes,
    electric, material, coef_keep, coef_curl, huygens_count, huygens_cells, band_tiles, radiation,
):
    cx, cy, cz = electric.shape[1:]
    hmax = huygens_cells.shape[-1]
    owned, row_tile = radiation.shape[0], radiation.shape[-1]
    n_gx, n_gy, n_af = sizes
    groups = n_gx * n_gy
    tiles = n_af * hmax // row_tile
    planes = cx + 2 * STEPS
    out_shape = (
        jax.ShapeDtypeStruct(electric.shape, f32),
        jax.ShapeDtypeStruct(electric.shape, f32),
        jax.ShapeDtypeStruct((STEPS, owned * row_tile), f32),
    )
    hbm = pl.BlockSpec(memory_space=pltpu.HBM)
    anyw = pl.BlockSpec(memory_space=pl.ANY)
    operands = [pltpu.with_memory_space_constraint(v, pltpu.HBM) for v in (electric, material, coef_keep, coef_curl)] + [huygens_count] + [
        pltpu.with_memory_space_constraint(v, pltpu.HBM) for v in (huygens_cells, band_tiles, radiation)]
    results = pl.pallas_call(
        functools.partial(kernel, sizes),
        out_shape=out_shape,
        in_specs=[hbm] * 8,
        out_specs=(anyw,) * 3,
        scratch_shapes=[
            pltpu.VMEM(electric.shape, f32),
            pltpu.VMEM(electric.shape, f32),
            pltpu.VMEM((STEPS, owned * row_tile), f32),
            pltpu.VMEM(material.shape, jnp.int32),
            pltpu.VMEM(coef_keep.shape, f32),
            pltpu.VMEM(coef_curl.shape, f32),
            pltpu.SMEM(huygens_count.shape, jnp.int32),
            pltpu.VMEM(huygens_cells.shape, jnp.int32),
            pltpu.SMEM(band_tiles.shape, jnp.int32),
            pltpu.VMEM((3, planes, 2, cy, 2 * cz), f32),
            pltpu.VMEM((3, planes, 2, cy, 2 * cz), f32),
            pltpu.VMEM((3, planes, 2, cy, 2 * cz), f32),
            pltpu.VMEM((3, planes, 2, cy, 2 * cz), f32),
            pltpu.VMEM((2, planes, 2, cy, 2 * cz), f32),
            pltpu.VMEM((2 * cz, 2 * cz), bf16),
            pltpu.VMEM((2 * cz, 2 * cz), bf16),
            pltpu.VMEM((cz, cx * cz), bf16),
            pltpu.VMEM((4, cy, 2 * cz), f32),
            pltpu.VMEM((2, 4, STEPS // 2, 2 * cy, cz), bf16),
            pltpu.VMEM((2, 4, cx // 4, 2 * cy, cz), bf16),
            pltpu.VMEM((2, 2 * cy, cz), bf16),
            pltpu.VMEM((2, 4, STEPS // 2, 2 * cy, cz), bf16),
            pltpu.VMEM((2, 4, planes // 4, 2 * cy, cz), bf16),
            pltpu.VMEM((2, 3, 3, 2, 2 * cy, cz), bf16),
            pltpu.VMEM((8, cz), f32),
            pltpu.VMEM((cz, hmax), jnp.bfloat16),
            pltpu.VMEM((cx * cy, hmax), f32),
            pltpu.VMEM((STEPS, tiles // 2, 16, row_tile), jnp.bfloat16),
            pltpu.VMEM(radiation.shape, jnp.bfloat16),
            pltpu.VMEM((groups, owned * STEPS, row_tile), f32),
            pltpu.SemaphoreType.DMA((len(STEPS_TO),)),
            pltpu.SemaphoreType.DMA((len(STEPS_TO),)),
            pltpu.SemaphoreType.DMA((STEPS, n_af)),
            pltpu.SemaphoreType.DMA((STEPS, n_af)),
            pltpu.SemaphoreType.DMA((groups,)),
            pltpu.SemaphoreType.DMA((groups,)),
            pltpu.SemaphoreType.DMA((8,)),
            pltpu.SemaphoreType.DMA((3,)),
        ],
        compiler_params=pltpu.CompilerParams(
            collective_id=0, has_side_effects=True, vmem_limit_bytes=24 * 1024 * 1024
        ),
    )(*operands)
    return pl.pallas_call(
        finish,
        out_shape=out_shape,
        in_specs=[anyw] * 3,
        out_specs=(hbm,) * 3,
        scratch_shapes=[pltpu.SemaphoreType.DMA((3,))],
        compiler_params=pltpu.CompilerParams(vmem_limit_bytes=16 * 1024 * 1024),
    )(*results)


def solution(mesh):
    placed = (
        P(None, "gx", "gy", "af"),
        P("gx", "gy", "af"),
        P(),
        P(),
        P("gx", "gy", "af"),
        P("gx", "gy", "af", None),
        P(("gx", "gy"), "af", None),
        P("af", ("gx", "gy"), None, None, None, None),
    )
    sizes = (mesh.shape["gx"], mesh.shape["gy"], mesh.shape["af"])
    return jax.shard_map(
        functools.partial(on_device, sizes),
        mesh=mesh,
        in_specs=placed,
        out_specs=(P(None, "gx", "gy", "af"), P(None, "gx", "gy", "af"), P(None, "af")),
        check_vma=False,
    )
```

```python
import functools
import itertools

import jax
import jax.numpy as jnp
from jax import lax
from jax.experimental import pallas as pl
from jax.experimental.pallas import tpu as pltpu
from jax.sharding import PartitionSpec as P

STEPS = 4
COURANT = 0.5
MESH = pl.DeviceIdType.MESH
f32, bf16 = jnp.float32, jnp.bfloat16

STEPS_TO = sorted(
    (d for d in itertools.product((-1, 0, 1), repeat=3) if any(d)),
    key=lambda d: (abs(d[2]), -abs(d[1]), abs(d[0])),
)
MESSAGES = [(d, 1) for d in STEPS_TO if d[1] and not d[2]] + [(d, 0) for d in STEPS_TO]


def kernel(
    sizes,
    electric_in, material_in, keep_in, curl_in, count_in, cells_in, band_in, radiation,
    e_end, h_end, pattern,
    e_out, h_out, material, coef_keep, coef_curl, count, cells, band,
    ef, gf, keep, gain, dz, ahead, behind, spread, low_mask,
    x_pack, y_pack, z_pack, zy_pack, x_ghost, y_ghost, z_ghost, zy_ghost,
    table, zhot, rhot, rows, weights, shares,
    send_sem, recv_sem, row_send, row_recv, share_send, share_recv, load_sem, store_sem,
):
    n_gx, n_gy, n_af = sizes
    groups = n_gx * n_gy
    gx, gy, af = lax.axis_index("gx"), lax.axis_index("gy"), lax.axis_index("af")
    me = (gx, gy, af)
    group = gx * n_gy + gy
    cx, cy, cz = e_out.shape[1:]
    hmax = cells.shape[-1]
    row_tile = radiation.shape[-1]
    tiles = hmax // row_tile
    owned, entries, comps = radiation.shape[0], radiation.shape[2], radiation.shape[3]

    def exists(step):
        ok = None
        for at, d, n in zip(me, step, sizes):
            if d:
                term = (at + d >= 0) if d < 0 else (at + d < n)
                ok = term if ok is None else jnp.logical_and(ok, term)
        return ok

    def place(step):
        return tuple(jnp.clip(at + d, 0, n - 1) if d else at for at, d, n in zip(me, step, sizes))

    def back(step):
        return tuple(-d for d in step)

    def af_peer(off):
        return (gx, gy, lax.rem(af + off, n_af))

    def group_peer(off):
        other = lax.rem(group + off, groups)
        return (other // n_gy, lax.rem(other, n_gy), af)

    def over_groups(body):
        if groups <= 16:
            for off in range(1, groups):
                body(off)
        else:
            def step(off, carry):
                body(off)
                return carry
            lax.fori_loop(1, groups, step, 0)

    halo = STEPS
    planes = cx + 2 * halo
    own = pl.ds(halo, cx)
    wide = 2 * cz
    loads = [
        pltpu.make_async_copy(src, dst, load_sem.at[i])
        for i, (src, dst) in enumerate((
            (electric_in, ef.at[:, own, 0, :, pl.ds(0, cz)]), (material_in, material),
            (keep_in, coef_keep), (curl_in, coef_curl), (cells_in, cells), (count_in, count),
            (band_in, band), (radiation, weights),
        ))
    ]
    stores = [
        pltpu.make_async_copy(src, dst, store_sem.at[i])
        for i, (src, dst) in enumerate(((e_out, e_end), (h_out, h_end)))
    ]

    barrier = pltpu.get_barrier_semaphore()
    for off in range(1, n_af):
        pl.semaphore_signal(barrier, inc=1, device_id=af_peer(off), device_id_type=MESH)
    over_groups(lambda off: pl.semaphore_signal(
        barrier, inc=1, device_id=group_peer(off), device_id_type=MESH))
    expected = jnp.int32(n_af - 1 + groups - 1)
    for step in STEPS_TO:
        if step[2] and (step[0] or step[1]):
            there = exists(step)
            expected = expected + there.astype(jnp.int32)

            @pl.when(there)
            def _(step=step):
                pl.semaphore_signal(barrier, inc=1, device_id=place(step), device_id_type=MESH)

    for load in loads[:-1]:
        load.start()

    lane = lax.broadcasted_iota(jnp.int32, (cy, cz), 1)
    sub = lax.broadcasted_iota(jnp.int32, (cy, cz), 0)
    low_rows = sub < halo
    edge = 2 * halo

    at = lax.broadcasted_iota(jnp.int32, (cz, cz), 0)
    to = lax.broadcasted_iota(jnp.int32, (cz, cz), 1)
    packed_at = jnp.where(to < halo, to, jnp.where(to >= cz - halo, to - (cz - edge), -cx * cz))
    for i in range(cx):
        spread[:, i * cz : (i + 1) * cz] = (at == packed_at + i * edge).astype(f32).astype(bf16)

    loads[0].wait()
    loads[1].wait()

    def own_plane(c, i):
        if c < 3:
            return ef[c, halo + i, 0, :, 0:cz]
        return material[i].astype(f32)

    for c in range(4):
        for j in range(cx // 4):
            four = [own_plane(c, 4 * j + r) for r in range(4)]
            turned = [pltpu.roll(four[1], halo, 0), pltpu.roll(four[3], halo, 0)]
            low = [jnp.where(low_rows, four[2 * r], turned[r]) for r in range(2)]
            high = [jnp.where(low_rows, turned[r], four[2 * r]) for r in range(2)]
            y_pack[0, c, j] = jnp.concatenate(low, axis=0).astype(bf16)
            y_pack[1, c, j] = jnp.concatenate(high, axis=0).astype(bf16)
    def message(m):
        (dx, dy, dz_), part = MESSAGES[m]
        side = 0 if dy < 0 else 1
        if dz_ and dy:
            src = zy_pack.at[side]
            dst = zy_ghost.at[0 if dz_ < 0 else 1, side, (0, 2, 1)[dx]]
        elif dz_:
            src = z_pack
            dst = z_ghost.at[0 if dz_ < 0 else 1, (0, 2, 1)[dx]]
        elif dy:
            n = 1 if dx else cx // 4
            first = cx // 4 - 1 if dx > 0 else 0
            to = (1, 0, cx // 4 + 1)[dx]
            what = pl.ds(3, 1) if part else pl.ds(0, 3)
            src = y_pack.at[side, what, pl.ds(first, n)]
            dst = y_ghost.at[side, what, pl.ds(to, n)]
        else:
            src = x_pack.at[1 if dx > 0 else 0]
            dst = x_ghost.at[0 if dx > 0 else 1]
        return pltpu.make_async_remote_copy(
            src_ref=src, dst_ref=dst, send_sem=send_sem.at[m], recv_sem=recv_sem.at[m],
            device_id=place((dx, dy, dz_)), device_id_type=MESH,
        )

    def send(wanted):
        for m, (step, _) in enumerate(MESSAGES):
            if wanted(step):
                @pl.when(exists(step))
                def _(m=m):
                    message(m).start()

    pl.semaphore_wait(barrier, expected)
    send(lambda d: d[1] and not d[2])
    for c in range(4):
        for side, first in ((0, 0), (1, cx - halo)):
            for j in range(halo // 2):
                pair = [own_plane(c, first + 2 * j), own_plane(c, first + 2 * j + 1)]
                x_pack[side, c, j] = jnp.concatenate(pair, axis=0).astype(bf16)
    send(lambda d: not d[1] and not d[2])
    lines = [jnp.concatenate([own_plane(c, i) for i in range(cx)], axis=1) for c in range(4)]
    ends = lax.dot_general(
        jnp.concatenate(lines, axis=0).astype(bf16), spread[...],
        (((1,), (1,)), ((), ())), preferred_element_type=f32)
    z_pack[...] = ends.reshape(2, 2 * cy, cz).astype(bf16)
    line = [ends[c * cy : (c + 1) * cy] for c in range(4)]
    turned = [pltpu.roll(line[1], halo, 0), pltpu.roll(line[3], halo, 0)]
    low = [jnp.where(low_rows, line[2 * r], turned[r]) for r in range(2)]
    high = [jnp.where(low_rows, turned[r], line[2 * r]) for r in range(2)]
    zy_pack[0] = jnp.concatenate(low, axis=0).astype(bf16)
    zy_pack[1] = jnp.concatenate(high, axis=0).astype(bf16)

    send(lambda d: d[2])
    loads[-1].start()

    def receive(wanted):
        for m, (step, part) in enumerate(MESSAGES):
            if wanted(step, part):
                @pl.when(exists(back(step)))
                def _(m=m):
                    message(m).wait_recv()

    outside = float(coef_keep.shape[1])
    pair_row = lax.broadcasted_iota(jnp.int32, (2 * cy, cz), 0)
    for step in STEPS_TO:
        @pl.when(jnp.logical_not(exists(back(step))))
        def _(step=step):
            dx, dy, dz_ = step
            nothing = jnp.zeros((2 * cy, cz), bf16)
            beyond = jnp.full((2 * cy, cz), outside, bf16)
            if dz_ and dy:
                first = cy + halo if dy < 0 else cy
                is_class = jnp.logical_and(pair_row >= first, pair_row < first + halo)
                zy_ghost[0 if dz_ < 0 else 1, 0 if dy < 0 else 1, (0, 2, 1)[dx]] = jnp.where(
                    is_class, outside, 0.0).astype(bf16)
            elif dz_:
                place_of = (0 if dz_ < 0 else 1, (0, 2, 1)[dx])
                z_ghost[place_of + (0,)] = nothing
                z_ghost[place_of + (1,)] = jnp.where(
                    pair_row >= cy, outside, 0.0).astype(bf16)
            elif dy:
                n = 1 if dx else cx // 4
                to = (1, 0, cx // 4 + 1)[dx]
                for c in range(4):
                    for j in range(to, to + n):
                        y_ghost[0 if dy < 0 else 1, c, j] = nothing if c < 3 else beyond
            else:
                for c in range(4):
                    for j in range(halo // 2):
                        x_ghost[0 if dx > 0 else 1, c, j] = nothing if c < 3 else beyond

    for load in loads[2:-1]:
        load.wait()
    table[...] = jnp.zeros_like(table)
    mats = coef_keep.shape[1]
    table[0:3, 0:mats] = coef_keep[...]
    table[3:6, 0:mats] = -COURANT * coef_curl[...]
    factors = [jnp.broadcast_to(table[c : c + 1, :], (cy, cz)) for c in range(6)]

    def picked_factors(classes):
        return [
            jnp.take_along_axis(row, classes, axis=1, mode="promise_in_bounds") for row in factors
        ]

    def set_factors(p, t, classes):
        for c, value in enumerate(picked_factors(classes)):
            (keep if c < 3 else gain)[c % 3, p, t, :, 0:cz] = value

    for i in range(cx):
        set_factors(halo + i, 0, material[i])
    row_at = lax.broadcasted_iota(jnp.int32, (wide, wide), 0)
    col_at = lax.broadcasted_iota(jnp.int32, (wide, wide), 1)
    same = (row_at == col_at).astype(f32)
    ahead[...] = ((row_at == lax.rem(col_at + 1, wide)).astype(f32) - same).astype(bf16)
    behind[...] = (same - (lax.rem(row_at + 1, wide) == col_at).astype(f32)).astype(bf16)
    deep = 4 * cz
    high = cx * cy // 4
    cell = jnp.broadcast_to(cells[...].reshape(1, hmax), (deep, hmax))
    wanted = lax.div(cell, high * cz) * cz + lax.rem(cell, cz)
    zhot[...] = (lax.broadcasted_iota(jnp.int32, (deep, hmax), 0) == wanted).astype(
        f32).astype(bf16)
    cell = jnp.broadcast_to(cells[...].reshape(1, hmax), (high, hmax))
    slot = lax.broadcasted_iota(jnp.int32, (high, hmax), 1)
    rhot[...] = jnp.logical_and(
        lax.broadcasted_iota(jnp.int32, (high, hmax), 0) == lax.rem(lax.div(cell, cz), high),
        slot < count[0, 0, 0],
    ).astype(f32)
    has_x = (gx > 0).astype(f32)
    has_y = (gy > 0).astype(f32)
    has_z = (af > 0).astype(f32)
    wide_lane = lax.broadcasted_iota(jnp.int32, (cy, wide), 1)
    wide_sub = lax.broadcasted_iota(jnp.int32, (cy, wide), 0)
    for x in range(2):
        for t in range(2):
            mask = jnp.where(wide_lane >= cz + cz // 2, has_z, 1.0)
            if t:
                mask = mask * jnp.where(wide_sub >= halo, has_y, 1.0)
            low_mask[2 * x + t] = mask * has_x if x else mask

    def as_classes(v):
        return v.astype(jnp.int32)

    def beside_y(c, use):
        for j in range(planes // 4):
            above = y_ghost[0, c, j].astype(f32)
            below = y_ghost[1, c, j].astype(f32)
            for r in range(2):
                up, down = above[r * cy : (r + 1) * cy], below[r * cy : (r + 1) * cy]
                use(4 * j + 2 * r, jnp.where(low_rows, up, down))
                use(4 * j + 2 * r + 1, pltpu.roll(jnp.where(low_rows, down, up), halo, 0))

    receive(lambda d, part: d[1] and part)
    beside_y(3, lambda p, v: set_factors(p, 1, as_classes(v)))

    receive(lambda d, part: d[0] and not d[1] and not d[2])
    for side, first in ((0, 0), (1, cx + halo)):
        for j in range(halo // 2):
            for c in range(4):
                pair = x_ghost[side, c, j].astype(f32)
                for r in range(2):
                    p = first + 2 * j + r
                    v = pair[r * cy : (r + 1) * cy]
                    if c < 3:
                        ef[c, p, 0, :, 0:cz] = v
                    else:
                        set_factors(p, 0, as_classes(v))

    receive(lambda d, part: d[2])
    from_above = lax.rem(lane, edge) < halo

    def ends_of(c, t, chunk):
        half = slice((c % 2) * cy, (c % 2 + 1) * cy)
        pair = slice((c // 2) * cy, (c // 2 + 1) * cy)

        def joined(dxi):
            if t == 0:
                above, below = [z_ghost[side, dxi, c // 2].astype(f32)[half] for side in range(2)]
                return jnp.where(from_above, above, below)
            out = []
            for side in range(2):
                up, down = [zy_ghost[side, y, dxi].astype(f32)[pair] for y in range(2)]
                if c % 2:
                    out.append(pltpu.roll(jnp.where(low_rows, down, up), halo, 0))
                else:
                    out.append(jnp.where(low_rows, up, down))
            return jnp.where(from_above, out[0], out[1])

        if chunk == 0:
            return joined(0)
        return jnp.where(lane < cz // 2, joined(1), joined(2))

    for chunk in range(2):
        if chunk == 0:
            blocks = [(0, [halo + i for i in range(cx)])]
        else:
            blocks = [(0, [cx + halo + i for i in range(halo)]), (cx - halo, list(range(halo)))]
        field = jnp.concatenate(
            [ends_of(c, t, chunk) for c in range(3) for t in range(2)], axis=0).astype(bf16)
        found = [picked_factors(as_classes(ends_of(3, t, chunk))) for t in range(2)]
        factor = jnp.concatenate([found[t][c] for c in range(6) for t in range(2)], axis=0)
        rough = factor.astype(bf16)
        rest = (factor - rough.astype(f32)).astype(bf16)
        for first, where_to in blocks:
            part = spread[:, first * cz : (first + len(where_to)) * cz]
            a = jnp.dot(field, part, preferred_element_type=f32)
            b = jnp.dot(rough, part, preferred_element_type=f32)
            b = b + jnp.dot(rest, part, preferred_element_type=f32)
            for i, p in enumerate(where_to):
                cols = slice(i * cz, (i + 1) * cz)
                for t in range(2):
                    for c in range(3):
                        at_row = (2 * c + t) * cy
                        ef[c, p, t, :, cz:wide] = a[at_row : at_row + cy, cols]
                        keep[c, p, t, :, cz:wide] = b[at_row : at_row + cy, cols]
                        at_row += 6 * cy
                        gain[c, p, t, :, cz:wide] = b[at_row : at_row + cy, cols]

    receive(lambda d, part: d[1] and not d[2] and not part)
    for c in range(3):
        def put(p, v, c=c):
            ef[c, p, 1, :, 0:cz] = v

        beside_y(c, put)

    def row_message(t, off):
        mine = rows.at[t, pl.ds(af * (tiles // 2), tiles // 2)]
        return pltpu.make_async_remote_copy(
            src_ref=mine, dst_ref=mine,
            send_sem=row_send.at[t, off], recv_sem=row_recv.at[t, off],
            device_id=af_peer(off), device_id_type=MESH,
        )

    def up_y(v):
        r = [pltpu.roll(tile, cy - 1, 0) for tile in v]
        last = wide_sub == cy - 1
        return [jnp.where(last, r[1], r[0]), jnp.where(last, r[0], r[1])]

    def down_y(v):
        r = [pltpu.roll(tile, 1, 0) for tile in v]
        first = wide_sub == 0
        return [jnp.where(first, r[1], r[0]), jnp.where(first, r[0], r[1])]

    def along_z(ref, c, first, n, matrix, width, tiles_y=2):
        v = ref[c, first : first + n, 0:tiles_y].reshape(n * tiles_y * cy, wide)
        rough = v.astype(bf16)
        rest = (v - rough.astype(f32)).astype(bf16)
        change = jnp.dot(rough, matrix[:, 0:width], preferred_element_type=f32)
        change = change + jnp.dot(rest, matrix[:, 0:width], preferred_element_type=f32)
        dz[c, first : first + n, 0:tiles_y, :, 0:width] = change.reshape(n, tiles_y, cy, width)

    def pick(compact, field):
        lines = []
        for k in range(3):
            if compact is not None:
                values = compact[k]
            else:
                values = field[k, halo : halo + cx, 0, :, 0:cz]
            quarters = values.reshape(4, high, cz)
            lines.append(jnp.concatenate([quarters[q] for q in range(4)], axis=1))
        column = jnp.dot(
            jnp.concatenate(lines, axis=0).astype(bf16), zhot[...], preferred_element_type=f32)
        return [
            jnp.sum(column[k * high : (k + 1) * high] * rhot[...], axis=0, keepdims=True)
            for k in range(3)
        ]

    def send_rows(t, electric_rows, magnetic_rows):
        picked = electric_rows + [-COURANT * row for row in magnetic_rows]
        picked = jnp.concatenate(picked + [jnp.zeros((8 - comps, hmax), f32)], axis=0)
        for q in range(tiles // 2):
            at = 2 * q * row_tile
            pair = [picked[:, at : at + row_tile], picked[:, at + row_tile : at + 2 * row_tile]]
            rows[t, af * (tiles // 2) + q] = jnp.concatenate(pair, axis=0).astype(bf16)
        for off in range(1, n_af):
            row_message(t, off).start()

    waiting = None
    for t in range(STEPS):
        first, last = t, planes - 2 - t
        end = t + 1 == STEPS
        for c in range(2):
            along_z(ef, c, first, last - first + 1, ahead, wide)
        for p in range(first, last + 1):
            ex, ey, ez = [[ef[c, p, y] for y in range(2)] for c in range(3)]
            ez_y, ex_y = up_y(ez), up_y(ex)
            for y in range(2):
                change = (
                    (ez_y[y] - ez[y]) - dz[1, p, y],
                    dz[0, p, y] - (ef[2, p + 1, y] - ez[y]),
                    (ef[1, p + 1, y] - ey[y]) - (ex_y[y] - ex[y]),
                )
                mask = low_mask[(2 if p < halo else 0) + y]
                if end and y:
                    needed, w = (0, 2), slice(0, cz)
                else:
                    needed, w = (0, 1, 2), slice(0, wide)
                for c in needed:
                    new = change[c][:, w] * mask[:, w]
                    if t:
                        new = gf[c, p, y, :, w] + new
                    gf[c, p, y, :, w] = new
        magnetic_rows = pick(None, gf)
        if waiting is not None:
            send_rows(*waiting)
        first = t + 1
        width = cz if end else wide
        for c in range(2):
            along_z(gf, c, first, last - first + 1, behind, width, 1 if end else 2)
        for p in range(first, last + 1):
            hx, hz = [[gf[c, p, y] for y in range(2)] for c in (0, 2)]
            hx_y, hz_y = down_y(hx), down_y(hz)
            for y in range(1 if end else 2):
                w = slice(0, width)
                change = (
                    (hz[y] - hz_y[y])[:, w] - dz[1, p, y, :, w],
                    dz[0, p, y, :, w] - (hz[y] - gf[2, p - 1, y])[:, w],
                    (gf[1, p, y] - gf[1, p - 1, y])[:, w] - (hx[y] - hx_y[y])[:, w],
                )
                for c in range(3):
                    new = keep[c, p, y, :, w] * ef[c, p, y, :, w] + gain[c, p, y, :, w] * change[c]
                    if end:
                        e_out[c, p - halo] = new
                        h_out[c, p - halo] = -COURANT * gf[c, p, 0, :, w]
                    else:
                        ef[c, p, y] = new
        electric_rows = pick(e_out if end else None, ef)
        if not end:
            waiting = (t, electric_rows, magnetic_rows)
    send_rows(STEPS - 1, electric_rows, magnetic_rows)
    stores[0].start()
    stores[1].start()

    loads[-1].wait()

    for t in range(STEPS):
        for off in range(1, n_af):
            row_message(t, off).wait_recv()
    sums = []
    for o in range(owned):
        segments, blocks = [], []
        for n in range(entries):
            tile = band[0, o, n]
            pairs = [rows[t, tile // 2].astype(f32) for t in range(STEPS)]
            odd = lax.rem(tile, 2)
            segments.append(jnp.concatenate(
                [jnp.where(odd == 1, pair[8:], pair[:8]) for pair in pairs], axis=0))
            blocks.append(weights[o, 0, n].reshape(comps * row_tile, row_tile))
        total = lax.dot_general(
            jnp.concatenate(segments, axis=1).astype(bf16),
            jnp.concatenate(blocks, axis=1),
            (((1,), (1,)), ((), ())),
            preferred_element_type=f32,
        )
        for t in range(STEPS):
            own = total[t * 8 : t * 8 + 1, 0:row_tile]
            for k in range(1, comps):
                own = own + total[t * 8 + k : t * 8 + k + 1, k * row_tile : (k + 1) * row_tile]
            sums.append(own)
    shares[group] = jnp.concatenate(sums, axis=0)

    def share_message(off):
        return pltpu.make_async_remote_copy(
            src_ref=shares.at[group], dst_ref=shares.at[group],
            send_sem=share_send.at[off], recv_sem=share_recv.at[off],
            device_id=group_peer(off), device_id_type=MESH,
        )

    over_groups(lambda off: share_message(off).start())
    for t in range(STEPS):
        for off in range(1, n_af):
            row_message(t, off).wait_send()
    for m in range(len(MESSAGES)):
        @pl.when(exists(MESSAGES[m][0]))
        def _(m=m):
            message(m).wait_send()
    stores[0].wait()
    stores[1].wait()
    over_groups(lambda off: share_message(off).wait_recv())
    total = jnp.sum(shares[...], axis=0)
    for o in range(owned):
        pattern[:, o * row_tile : (o + 1) * row_tile] = total[o * STEPS : (o + 1) * STEPS]

    over_groups(lambda off: share_message(off).wait_send())


def finish(e_in, h_in, p_in, e_out, h_out, p_out, sem):
    stores = [
        pltpu.make_async_copy(src, dst, sem.at[i])
        for i, (src, dst) in enumerate(((p_in, p_out), (e_in, e_out), (h_in, h_out)))
    ]
    for store in stores:
        store.start()
    for store in stores:
        store.wait()


def on_device(
    sizes,
    electric, material, coef_keep, coef_curl, huygens_count, huygens_cells, band_tiles, radiation,
):
    cx, cy, cz = electric.shape[1:]
    hmax = huygens_cells.shape[-1]
    owned, row_tile = radiation.shape[0], radiation.shape[-1]
    n_gx, n_gy, n_af = sizes
    groups = n_gx * n_gy
    tiles = n_af * hmax // row_tile
    planes = cx + 2 * STEPS
    out_shape = (
        jax.ShapeDtypeStruct(electric.shape, f32),
        jax.ShapeDtypeStruct(electric.shape, f32),
        jax.ShapeDtypeStruct((STEPS, owned * row_tile), f32),
    )
    hbm = pl.BlockSpec(memory_space=pltpu.HBM)
    anyw = pl.BlockSpec(memory_space=pl.ANY)
    operands = [pltpu.with_memory_space_constraint(v, pltpu.HBM) for v in (electric, material, coef_keep, coef_curl)] + [huygens_count] + [
        pltpu.with_memory_space_constraint(v, pltpu.HBM) for v in (huygens_cells, band_tiles, radiation)]
    results = pl.pallas_call(
        functools.partial(kernel, sizes),
        out_shape=out_shape,
        in_specs=[hbm] * 8,
        out_specs=(anyw, anyw, pl.BlockSpec(memory_space=pltpu.VMEM)),
        scratch_shapes=[
            pltpu.VMEM(electric.shape, f32),
            pltpu.VMEM(electric.shape, f32),
            pltpu.VMEM(material.shape, jnp.int32),
            pltpu.VMEM(coef_keep.shape, f32),
            pltpu.VMEM(coef_curl.shape, f32),
            pltpu.SMEM(huygens_count.shape, jnp.int32),
            pltpu.VMEM(huygens_cells.shape, jnp.int32),
            pltpu.SMEM(band_tiles.shape, jnp.int32),
            pltpu.VMEM((3, planes, 2, cy, 2 * cz), f32),
            pltpu.VMEM((3, planes, 2, cy, 2 * cz), f32),
            pltpu.VMEM((3, planes, 2, cy, 2 * cz), f32),
            pltpu.VMEM((3, planes, 2, cy, 2 * cz), f32),
            pltpu.VMEM((2, planes, 2, cy, 2 * cz), f32),
            pltpu.VMEM((2 * cz, 2 * cz), bf16),
            pltpu.VMEM((2 * cz, 2 * cz), bf16),
            pltpu.VMEM((cz, cx * cz), bf16),
            pltpu.VMEM((4, cy, 2 * cz), f32),
            pltpu.VMEM((2, 4, STEPS // 2, 2 * cy, cz), bf16),
            pltpu.VMEM((2, 4, cx // 4, 2 * cy, cz), bf16),
            pltpu.VMEM((2, 2 * cy, cz), bf16),
            pltpu.VMEM((2, 2 * cy, cz), bf16),
            pltpu.VMEM((2, 4, STEPS // 2, 2 * cy, cz), bf16),
            pltpu.VMEM((2, 4, planes // 4, 2 * cy, cz), bf16),
            pltpu.VMEM((2, 3, 2, 2 * cy, cz), bf16),
            pltpu.VMEM((2, 2, 3, 2 * cy, cz), bf16),
            pltpu.VMEM((8, cz), f32),
            pltpu.VMEM((4 * cz, hmax), bf16),
            pltpu.VMEM((cx * cy // 4, hmax), f32),
            pltpu.VMEM((STEPS, tiles // 2, 16, row_tile), jnp.bfloat16),
            pltpu.VMEM(radiation.shape, jnp.bfloat16),
            pltpu.VMEM((groups, owned * STEPS, row_tile), f32),
            pltpu.SemaphoreType.DMA((len(MESSAGES),)),
            pltpu.SemaphoreType.DMA((len(MESSAGES),)),
            pltpu.SemaphoreType.DMA((STEPS, n_af)),
            pltpu.SemaphoreType.DMA((STEPS, n_af)),
            pltpu.SemaphoreType.DMA((groups,)),
            pltpu.SemaphoreType.DMA((groups,)),
            pltpu.SemaphoreType.DMA((8,)),
            pltpu.SemaphoreType.DMA((2,)),
        ],
        compiler_params=pltpu.CompilerParams(
            collective_id=0, has_side_effects=True, vmem_limit_bytes=24 * 1024 * 1024
        ),
    )(*operands)
    return pl.pallas_call(
        finish,
        out_shape=out_shape,
        in_specs=[anyw] * 3,
        out_specs=(hbm,) * 3,
        scratch_shapes=[pltpu.SemaphoreType.DMA((3,))],
        compiler_params=pltpu.CompilerParams(vmem_limit_bytes=16 * 1024 * 1024),
    )(*results)


def solution(mesh):
    placed = (
        P(None, "gx", "gy", "af"),
        P("gx", "gy", "af"),
        P(),
        P(),
        P("gx", "gy", "af"),
        P("gx", "gy", "af", None),
        P(("gx", "gy"), "af", None),
        P("af", ("gx", "gy"), None, None, None, None),
    )
    sizes = (mesh.shape["gx"], mesh.shape["gy"], mesh.shape["af"])
    return jax.shard_map(
        functools.partial(on_device, sizes),
        mesh=mesh,
        in_specs=placed,
        out_specs=(P(None, "gx", "gy", "af"), P(None, "gx", "gy", "af"), P(None, "af")),
        check_vma=False,
    )
```

```python
import functools
import itertools

import jax
import jax.numpy as jnp
from jax import lax
from jax.experimental import pallas as pl
from jax.experimental.pallas import tpu as pltpu
from jax.sharding import PartitionSpec as P

STEPS = 4
COURANT = 0.5
TURNED = 8
MESH = pl.DeviceIdType.MESH
f32, bf16 = jnp.float32, jnp.bfloat16

STEPS_TO = sorted(
    (d for d in itertools.product((-1, 0, 1), repeat=3) if any(d)),
    key=lambda d: (abs(d[2]), -abs(d[1]), abs(d[0])),
)
MESSAGES = [(d, 1) for d in STEPS_TO if d[1] and not d[2]] + [(d, 0) for d in STEPS_TO]


def kernel(
    sizes,
    electric_in, material_in, keep_in, curl_in, count_in, cells_in, band_in, radiation,
    e_end, h_end, pattern,
    e_out, h_out, material, coef_keep, coef_curl, count, cells, band,
    ef, gf, keep, gain, dz, ahead, behind, spread, low_mask,
    x_pack, y_pack, z_pack, zy_pack, x_ghost, y_ghost, z_ghost, zy_ghost,
    table, zhot, rhot, rows, weights, shares,
    send_sem, recv_sem, row_send, row_recv, share_send, share_recv, load_sem, store_sem,
):
    n_gx, n_gy, n_af = sizes
    groups = n_gx * n_gy
    gx, gy, af = lax.axis_index("gx"), lax.axis_index("gy"), lax.axis_index("af")
    me = (gx, gy, af)
    group = gx * n_gy + gy
    cx, cy, cz = e_out.shape[1:]
    hmax = cells.shape[-1]
    row_tile = radiation.shape[-1]
    tiles = hmax // row_tile
    owned, entries, comps = radiation.shape[0], radiation.shape[2], radiation.shape[3]

    def exists(step):
        ok = None
        for at, d, n in zip(me, step, sizes):
            if d:
                term = (at + d >= 0) if d < 0 else (at + d < n)
                ok = term if ok is None else jnp.logical_and(ok, term)
        return ok

    def place(step):
        return tuple(jnp.clip(at + d, 0, n - 1) if d else at for at, d, n in zip(me, step, sizes))

    def back(step):
        return tuple(-d for d in step)

    def af_peer(off):
        return (gx, gy, lax.rem(af + off, n_af))

    def group_peer(off):
        other = lax.rem(group + off, groups)
        return (other // n_gy, lax.rem(other, n_gy), af)

    def over_groups(body):
        if groups <= 16:
            for off in range(1, groups):
                body(off)
        else:
            def step(off, carry):
                body(off)
                return carry
            lax.fori_loop(1, groups, step, 0)

    halo = STEPS
    planes = cx + 2 * halo
    own = pl.ds(halo, cx)
    wide = 2 * cz
    loads = [
        pltpu.make_async_copy(src, dst, load_sem.at[i])
        for i, (src, dst) in enumerate((
            (electric_in, ef.at[:, own, 0, :, pl.ds(0, cz)]), (material_in, material),
            (keep_in, coef_keep), (curl_in, coef_curl), (cells_in, cells), (count_in, count),
            (band_in, band), (radiation, weights),
        ))
    ]
    stores = [
        pltpu.make_async_copy(src, dst, store_sem.at[i])
        for i, (src, dst) in enumerate(((e_out, e_end), (h_out, h_end)))
    ]

    barrier = pltpu.get_barrier_semaphore()
    for off in range(1, n_af):
        pl.semaphore_signal(barrier, inc=1, device_id=af_peer(off), device_id_type=MESH)
    over_groups(lambda off: pl.semaphore_signal(
        barrier, inc=1, device_id=group_peer(off), device_id_type=MESH))
    expected = jnp.int32(n_af - 1 + groups - 1)
    for step in STEPS_TO:
        if step[2] and (step[0] or step[1]):
            there = exists(step)
            expected = expected + there.astype(jnp.int32)

            @pl.when(there)
            def _(step=step):
                pl.semaphore_signal(barrier, inc=1, device_id=place(step), device_id_type=MESH)

    for load in loads[:-1]:
        load.start()

    lane = lax.broadcasted_iota(jnp.int32, (cy, cz), 1)
    sub = lax.broadcasted_iota(jnp.int32, (cy, cz), 0)
    low_rows = sub < halo
    edge = 2 * halo

    at = lax.broadcasted_iota(jnp.int32, (cz, cz), 0)
    to = lax.broadcasted_iota(jnp.int32, (cz, cz), 1)
    packed_at = jnp.where(to < halo, to, jnp.where(to >= cz - halo, to - (cz - edge), -cx * cz))
    for i in range(cx):
        spread[:, i * cz : (i + 1) * cz] = (at == packed_at + i * edge).astype(f32).astype(bf16)

    loads[0].wait()
    loads[1].wait()

    def own_plane(c, i):
        if c < 3:
            return ef[c, halo + i, 0, :, 0:cz]
        return material[i].astype(f32)

    for c in range(4):
        for j in range(cx // 4):
            four = [own_plane(c, 4 * j + r) for r in range(4)]
            turned = [pltpu.roll(four[1], halo, 0), pltpu.roll(four[3], halo, 0)]
            low = [jnp.where(low_rows, four[2 * r], turned[r]) for r in range(2)]
            high = [jnp.where(low_rows, turned[r], four[2 * r]) for r in range(2)]
            y_pack[0, c, j] = jnp.concatenate(low, axis=0).astype(bf16)
            y_pack[1, c, j] = jnp.concatenate(high, axis=0).astype(bf16)
    def message(m):
        (dx, dy, dz_), part = MESSAGES[m]
        side = 0 if dy < 0 else 1
        if dz_ and dy:
            src = zy_pack.at[side]
            dst = zy_ghost.at[0 if dz_ < 0 else 1, side, (0, 2, 1)[dx]]
        elif dz_:
            src = z_pack
            dst = z_ghost.at[0 if dz_ < 0 else 1, (0, 2, 1)[dx]]
        elif dy:
            n = 1 if dx else cx // 4
            first = cx // 4 - 1 if dx > 0 else 0
            to = (1, 0, cx // 4 + 1)[dx]
            what = pl.ds(3, 1) if part else pl.ds(0, 3)
            src = y_pack.at[side, what, pl.ds(first, n)]
            dst = y_ghost.at[side, what, pl.ds(to, n)]
        else:
            src = x_pack.at[1 if dx > 0 else 0]
            dst = x_ghost.at[0 if dx > 0 else 1]
        return pltpu.make_async_remote_copy(
            src_ref=src, dst_ref=dst, send_sem=send_sem.at[m], recv_sem=recv_sem.at[m],
            device_id=place((dx, dy, dz_)), device_id_type=MESH,
        )

    def send(wanted):
        for m, (step, _) in enumerate(MESSAGES):
            if wanted(step):
                @pl.when(exists(step))
                def _(m=m):
                    message(m).start()

    pl.semaphore_wait(barrier, expected)
    send(lambda d: d[1] and not d[2])
    for c in range(4):
        for side, first in ((0, 0), (1, cx - halo)):
            for j in range(halo // 2):
                pair = [own_plane(c, first + 2 * j), own_plane(c, first + 2 * j + 1)]
                x_pack[side, c, j] = jnp.concatenate(pair, axis=0).astype(bf16)
    send(lambda d: not d[1] and not d[2])
    lines = [jnp.concatenate([own_plane(c, i) for i in range(cx)], axis=1) for c in range(4)]
    ends = lax.dot_general(
        jnp.concatenate(lines, axis=0).astype(bf16), spread[...],
        (((1,), (1,)), ((), ())), preferred_element_type=f32)
    z_pack[...] = ends.reshape(2, 2 * cy, cz).astype(bf16)
    line = [ends[c * cy : (c + 1) * cy] for c in range(4)]
    turned = [pltpu.roll(line[1], halo, 0), pltpu.roll(line[3], halo, 0)]
    low = [jnp.where(low_rows, line[2 * r], turned[r]) for r in range(2)]
    high = [jnp.where(low_rows, turned[r], line[2 * r]) for r in range(2)]
    zy_pack[0] = jnp.concatenate(low, axis=0).astype(bf16)
    zy_pack[1] = jnp.concatenate(high, axis=0).astype(bf16)

    send(lambda d: d[2])
    loads[-1].start()

    def receive(wanted):
        for m, (step, part) in enumerate(MESSAGES):
            if wanted(step, part):
                @pl.when(exists(back(step)))
                def _(m=m):
                    message(m).wait_recv()

    outside = float(coef_keep.shape[1])
    pair_row = lax.broadcasted_iota(jnp.int32, (2 * cy, cz), 0)
    for step in STEPS_TO:
        @pl.when(jnp.logical_not(exists(back(step))))
        def _(step=step):
            dx, dy, dz_ = step
            nothing = jnp.zeros((2 * cy, cz), bf16)
            beyond = jnp.full((2 * cy, cz), outside, bf16)
            if dz_ and dy:
                first = cy + halo if dy < 0 else cy
                is_class = jnp.logical_and(pair_row >= first, pair_row < first + halo)
                zy_ghost[0 if dz_ < 0 else 1, 0 if dy < 0 else 1, (0, 2, 1)[dx]] = jnp.where(
                    is_class, outside, 0.0).astype(bf16)
            elif dz_:
                place_of = (0 if dz_ < 0 else 1, (0, 2, 1)[dx])
                z_ghost[place_of + (0,)] = nothing
                z_ghost[place_of + (1,)] = jnp.where(
                    pair_row >= cy, outside, 0.0).astype(bf16)
            elif dy:
                n = 1 if dx else cx // 4
                to = (1, 0, cx // 4 + 1)[dx]
                for c in range(4):
                    for j in range(to, to + n):
                        y_ghost[0 if dy < 0 else 1, c, j] = nothing if c < 3 else beyond
            else:
                for c in range(4):
                    for j in range(halo // 2):
                        x_ghost[0 if dx > 0 else 1, c, j] = nothing if c < 3 else beyond

    for load in loads[2:-1]:
        load.wait()
    table[...] = jnp.zeros_like(table)
    mats = coef_keep.shape[1]
    table[0:3, 0:mats] = coef_keep[...]
    table[3:6, 0:mats] = -COURANT * coef_curl[...]
    factors = [jnp.broadcast_to(table[c : c + 1, :], (cy, cz)) for c in range(6)]

    def picked_factors(classes):
        return [
            jnp.take_along_axis(row, classes, axis=1, mode="promise_in_bounds") for row in factors
        ]

    def set_factors(p, t, classes):
        for c, value in enumerate(picked_factors(classes)):
            (keep if c < 3 else gain)[c % 3, p, t, :, 0:cz] = value

    for i in range(cx):
        set_factors(halo + i, 0, material[i])
    row_at = lax.broadcasted_iota(jnp.int32, (wide, wide), 0)
    col_at = lax.broadcasted_iota(jnp.int32, (wide, wide), 1)
    same = (row_at == col_at).astype(f32)
    ahead[...] = ((row_at == lax.rem(col_at + 1, wide)).astype(f32) - same).astype(bf16)
    behind[...] = (same - (lax.rem(row_at + 1, wide) == col_at).astype(f32)).astype(bf16)
    deep = 4 * cz
    high = cx * cy // 4
    cell = jnp.broadcast_to(cells[...].reshape(1, hmax), (deep, hmax))
    wanted = lax.div(cell, high * cz) * cz + lax.rem(cell, cz)
    zhot[...] = (lax.broadcasted_iota(jnp.int32, (deep, hmax), 0) == wanted).astype(
        f32).astype(bf16)
    cell = jnp.broadcast_to(cells[...].reshape(1, hmax), (high, hmax))
    slot = lax.broadcasted_iota(jnp.int32, (high, hmax), 1)
    rhot[...] = jnp.logical_and(
        lax.broadcasted_iota(jnp.int32, (high, hmax), 0) == lax.rem(lax.div(cell, cz), high),
        slot < count[0, 0, 0],
    ).astype(f32)
    has_x = (gx > 0).astype(f32)
    has_y = (gy > 0).astype(f32)
    has_z = (af > 0).astype(f32)
    wide_lane = lax.broadcasted_iota(jnp.int32, (cy, wide), 1)
    wide_sub = lax.broadcasted_iota(jnp.int32, (cy, wide), 0)
    for x in range(2):
        for t in range(2):
            mask = jnp.where(wide_lane >= cz + cz // 2, has_z, 1.0)
            if t:
                mask = mask * jnp.where(wide_sub >= halo, has_y, 1.0)
            low_mask[2 * x + t] = mask * has_x if x else mask

    def as_classes(v):
        return v.astype(jnp.int32)

    def beside_y(c, use):
        for j in range(planes // 4):
            above = y_ghost[0, c, j].astype(f32)
            below = y_ghost[1, c, j].astype(f32)
            for r in range(2):
                up, down = above[r * cy : (r + 1) * cy], below[r * cy : (r + 1) * cy]
                use(4 * j + 2 * r, jnp.where(low_rows, up, down))
                use(4 * j + 2 * r + 1, pltpu.roll(jnp.where(low_rows, down, up), halo, 0))

    receive(lambda d, part: d[1] and part)
    beside_y(3, lambda p, v: set_factors(p, 1, as_classes(v)))

    receive(lambda d, part: d[0] and not d[1] and not d[2])
    for side, first in ((0, 0), (1, cx + halo)):
        for j in range(halo // 2):
            for c in range(4):
                pair = x_ghost[side, c, j].astype(f32)
                for r in range(2):
                    p = first + 2 * j + r
                    v = pair[r * cy : (r + 1) * cy]
                    if c < 3:
                        ef[c, p, 0, :, 0:cz] = v
                    else:
                        set_factors(p, 0, as_classes(v))

    receive(lambda d, part: d[1] and not d[2] and not part)
    for c in range(3):
        def put(p, v, c=c):
            ef[c, p, 1, :, 0:cz] = v

        beside_y(c, put)

    receive(lambda d, part: d[2])
    from_above = lax.rem(lane, edge) < halo

    def ends_of(c, t, chunk):
        half = slice((c % 2) * cy, (c % 2 + 1) * cy)
        pair = slice((c // 2) * cy, (c // 2 + 1) * cy)

        def joined(dxi):
            if t == 0:
                above, below = [z_ghost[side, dxi, c // 2].astype(f32)[half] for side in range(2)]
                return jnp.where(from_above, above, below)
            out = []
            for side in range(2):
                up, down = [zy_ghost[side, y, dxi].astype(f32)[pair] for y in range(2)]
                if c % 2:
                    out.append(pltpu.roll(jnp.where(low_rows, down, up), halo, 0))
                else:
                    out.append(jnp.where(low_rows, up, down))
            return jnp.where(from_above, out[0], out[1])

        if chunk == 0:
            return joined(0)
        return jnp.where(lane < cz // 2, joined(1), joined(2))

    for chunk in range(2):
        if chunk == 0:
            blocks = [(0, [halo + i for i in range(cx)])]
        else:
            blocks = [(0, [cx + halo + i for i in range(halo)]), (cx - halo, list(range(halo)))]
        field = jnp.concatenate(
            [ends_of(c, t, chunk) for c in range(3) for t in range(2)], axis=0).astype(bf16)
        found = [picked_factors(as_classes(ends_of(3, t, chunk))) for t in range(2)]
        factor = jnp.concatenate([found[t][c] for c in range(6) for t in range(2)], axis=0)
        rough = factor.astype(bf16)
        rest = (factor - rough.astype(f32)).astype(bf16)
        for first, where_to in blocks:
            part = spread[:, first * cz : (first + len(where_to)) * cz]
            a = jnp.dot(field, part, preferred_element_type=f32)
            b = jnp.dot(rough, part, preferred_element_type=f32)
            b = b + jnp.dot(rest, part, preferred_element_type=f32)
            for i, p in enumerate(where_to):
                cols = slice(i * cz, (i + 1) * cz)
                for t in range(2):
                    for c in range(3):
                        at_row = (2 * c + t) * cy
                        ef[c, p, t, :, cz:wide] = a[at_row : at_row + cy, cols]
                        keep[c, p, t, :, cz:wide] = b[at_row : at_row + cy, cols]
                        at_row += 6 * cy
                        gain[c, p, t, :, cz:wide] = b[at_row : at_row + cy, cols]

    def row_message(t, off):
        mine = rows.at[t, pl.ds(af * (tiles // 2), tiles // 2)]
        return pltpu.make_async_remote_copy(
            src_ref=mine, dst_ref=mine,
            send_sem=row_send.at[t, off], recv_sem=row_recv.at[t, off],
            device_id=af_peer(off), device_id_type=MESH,
        )

    def up_y(v):
        r = [pltpu.roll(tile, cy - 1, 0) for tile in v]
        last = wide_sub == cy - 1
        return [jnp.where(last, r[1], r[0]), jnp.where(last, r[0], r[1])]

    def down_y(v):
        r = [pltpu.roll(tile, 1, 0) for tile in v]
        first = wide_sub == 0
        return [jnp.where(first, r[1], r[0]), jnp.where(first, r[0], r[1])]

    def along_z(ref, c, first, n, matrix, width, tiles_y=2):
        v = ref[c, first : first + n, 0:tiles_y].reshape(n * tiles_y * cy, wide)
        rough = v.astype(bf16)
        rest = (v - rough.astype(f32)).astype(bf16)
        change = jnp.dot(rough, matrix[:, 0:width], preferred_element_type=f32)
        change = change + jnp.dot(rest, matrix[:, 0:width], preferred_element_type=f32)
        dz[c, first : first + n, 0:tiles_y, :, 0:width] = change.reshape(n, tiles_y, cy, width)

    def pick(compact, field):
        lines = []
        for k in range(3):
            if compact is not None:
                values = compact[k]
            else:
                values = field[k, halo : halo + cx, 0, :, 0:cz]
            quarters = values.reshape(4, high, cz)
            lines.append(jnp.concatenate([quarters[q] for q in range(4)], axis=1))
        column = jnp.dot(
            jnp.concatenate(lines, axis=0).astype(bf16), zhot[...], preferred_element_type=f32)
        return [
            jnp.sum(column[k * high : (k + 1) * high] * rhot[...], axis=0, keepdims=True)
            for k in range(3)
        ]

    def send_rows(t, electric_rows, magnetic_rows):
        picked = electric_rows + [-COURANT * row for row in magnetic_rows]
        picked = jnp.concatenate(picked + [jnp.zeros((8 - comps, hmax), f32)], axis=0)
        for q in range(tiles // 2):
            at = 2 * q * row_tile
            pair = [picked[:, at : at + row_tile], picked[:, at + row_tile : at + 2 * row_tile]]
            rows[t, af * (tiles // 2) + q] = jnp.concatenate(pair, axis=0).astype(bf16)
        for off in range(1, n_af):
            row_message(t, off).start()

    waiting = None
    for t in range(STEPS):
        first, last = t, planes - 2 - t
        end = t + 1 == STEPS
        for c in range(2):
            along_z(ef, c, first, last - first + 1 - TURNED, ahead, wide)
        for p in range(first, last + 1):
            ex, ey, ez = [[ef[c, p, y] for y in range(2)] for c in range(3)]
            ez_y, ex_y = up_y(ez), up_y(ex)
            for y in range(2):
                if p > last - TURNED:
                    z_x, z_y = [pltpu.roll(v[y], wide - 1, 1) - v[y] for v in (ex, ey)]
                else:
                    z_x, z_y = dz[0, p, y], dz[1, p, y]
                change = (
                    (ez_y[y] - ez[y]) - z_y,
                    z_x - (ef[2, p + 1, y] - ez[y]),
                    (ef[1, p + 1, y] - ey[y]) - (ex_y[y] - ex[y]),
                )
                mask = low_mask[(2 if p < halo else 0) + y]
                if end and y:
                    needed, w = (0, 2), slice(0, cz)
                else:
                    needed, w = (0, 1, 2), slice(0, wide)
                for c in needed:
                    new = change[c][:, w] * mask[:, w]
                    if t:
                        new = gf[c, p, y, :, w] + new
                    gf[c, p, y, :, w] = new
        magnetic_rows = pick(None, gf)
        if waiting is not None:
            send_rows(*waiting)
        first = t + 1
        width = cz if end else wide
        for c in range(2):
            along_z(gf, c, first, last - first + 1 - TURNED, behind, width, 1 if end else 2)
        for p in range(first, last + 1):
            hx, hz = [[gf[c, p, y] for y in range(2)] for c in (0, 2)]
            hx_y, hz_y = down_y(hx), down_y(hz)
            for y in range(1 if end else 2):
                w = slice(0, width)
                if p > last - TURNED:
                    z_x, z_y = [
                        (v - pltpu.roll(v, 1, 1))[:, w] for v in (hx[y], gf[1, p, y])]
                else:
                    z_x, z_y = dz[0, p, y, :, w], dz[1, p, y, :, w]
                change = (
                    (hz[y] - hz_y[y])[:, w] - z_y,
                    z_x - (hz[y] - gf[2, p - 1, y])[:, w],
                    (gf[1, p, y] - gf[1, p - 1, y])[:, w] - (hx[y] - hx_y[y])[:, w],
                )
                for c in range(3):
                    new = keep[c, p, y, :, w] * ef[c, p, y, :, w] + gain[c, p, y, :, w] * change[c]
                    if end:
                        e_out[c, p - halo] = new
                        h_out[c, p - halo] = -COURANT * gf[c, p, 0, :, w]
                    else:
                        ef[c, p, y] = new
        electric_rows = pick(e_out if end else None, ef)
        if not end:
            waiting = (t, electric_rows, magnetic_rows)
    send_rows(STEPS - 1, electric_rows, magnetic_rows)
    stores[0].start()
    stores[1].start()

    loads[-1].wait()

    for t in range(STEPS):
        for off in range(1, n_af):
            row_message(t, off).wait_recv()
    sums = []
    for o in range(owned):
        segments, blocks = [], []
        for n in range(entries):
            tile = band[0, o, n]
            pairs = [rows[t, tile // 2].astype(f32) for t in range(STEPS)]
            odd = lax.rem(tile, 2)
            segments.append(jnp.concatenate(
                [jnp.where(odd == 1, pair[8:], pair[:8]) for pair in pairs], axis=0))
            blocks.append(weights[o, 0, n].reshape(comps * row_tile, row_tile))
        total = lax.dot_general(
            jnp.concatenate(segments, axis=1).astype(bf16),
            jnp.concatenate(blocks, axis=1),
            (((1,), (1,)), ((), ())),
            preferred_element_type=f32,
        )
        for t in range(STEPS):
            own = total[t * 8 : t * 8 + 1, 0:row_tile]
            for k in range(1, comps):
                own = own + total[t * 8 + k : t * 8 + k + 1, k * row_tile : (k + 1) * row_tile]
            sums.append(own)
    shares[group] = jnp.concatenate(sums, axis=0)

    def share_message(off):
        return pltpu.make_async_remote_copy(
            src_ref=shares.at[group], dst_ref=shares.at[group],
            send_sem=share_send.at[off], recv_sem=share_recv.at[off],
            device_id=group_peer(off), device_id_type=MESH,
        )

    over_groups(lambda off: share_message(off).start())
    for t in range(STEPS):
        for off in range(1, n_af):
            row_message(t, off).wait_send()
    for m in range(len(MESSAGES)):
        @pl.when(exists(MESSAGES[m][0]))
        def _(m=m):
            message(m).wait_send()
    stores[0].wait()
    stores[1].wait()
    over_groups(lambda off: share_message(off).wait_recv())
    total = jnp.sum(shares[...], axis=0)
    for o in range(owned):
        pattern[:, o * row_tile : (o + 1) * row_tile] = total[o * STEPS : (o + 1) * STEPS]

    over_groups(lambda off: share_message(off).wait_send())


def finish(e_in, h_in, p_in, e_out, h_out, p_out, sem):
    stores = [
        pltpu.make_async_copy(src, dst, sem.at[i])
        for i, (src, dst) in enumerate(((p_in, p_out), (e_in, e_out), (h_in, h_out)))
    ]
    for store in stores:
        store.start()
    for store in stores:
        store.wait()


def on_device(
    sizes,
    electric, material, coef_keep, coef_curl, huygens_count, huygens_cells, band_tiles, radiation,
):
    cx, cy, cz = electric.shape[1:]
    hmax = huygens_cells.shape[-1]
    owned, row_tile = radiation.shape[0], radiation.shape[-1]
    n_gx, n_gy, n_af = sizes
    groups = n_gx * n_gy
    tiles = n_af * hmax // row_tile
    planes = cx + 2 * STEPS
    out_shape = (
        jax.ShapeDtypeStruct(electric.shape, f32),
        jax.ShapeDtypeStruct(electric.shape, f32),
        jax.ShapeDtypeStruct((STEPS, owned * row_tile), f32),
    )
    hbm = pl.BlockSpec(memory_space=pltpu.HBM)
    anyw = pl.BlockSpec(memory_space=pl.ANY)
    operands = [pltpu.with_memory_space_constraint(v, pltpu.HBM) for v in (electric, material, coef_keep, coef_curl)] + [huygens_count] + [
        pltpu.with_memory_space_constraint(v, pltpu.HBM) for v in (huygens_cells, band_tiles, radiation)]
    results = pl.pallas_call(
        functools.partial(kernel, sizes),
        out_shape=out_shape,
        in_specs=[hbm] * 8,
        out_specs=(anyw, anyw, pl.BlockSpec(memory_space=pltpu.VMEM)),
        scratch_shapes=[
            pltpu.VMEM(electric.shape, f32),
            pltpu.VMEM(electric.shape, f32),
            pltpu.VMEM(material.shape, jnp.int32),
            pltpu.VMEM(coef_keep.shape, f32),
            pltpu.VMEM(coef_curl.shape, f32),
            pltpu.SMEM(huygens_count.shape, jnp.int32),
            pltpu.VMEM(huygens_cells.shape, jnp.int32),
            pltpu.SMEM(band_tiles.shape, jnp.int32),
            pltpu.VMEM((3, planes, 2, cy, 2 * cz), f32),
            pltpu.VMEM((3, planes, 2, cy, 2 * cz), f32),
            pltpu.VMEM((3, planes, 2, cy, 2 * cz), f32),
            pltpu.VMEM((3, planes, 2, cy, 2 * cz), f32),
            pltpu.VMEM((2, planes, 2, cy, 2 * cz), f32),
            pltpu.VMEM((2 * cz, 2 * cz), bf16),
            pltpu.VMEM((2 * cz, 2 * cz), bf16),
            pltpu.VMEM((cz, cx * cz), bf16),
            pltpu.VMEM((4, cy, 2 * cz), f32),
            pltpu.VMEM((2, 4, STEPS // 2, 2 * cy, cz), bf16),
            pltpu.VMEM((2, 4, cx // 4, 2 * cy, cz), bf16),
            pltpu.VMEM((2, 2 * cy, cz), bf16),
            pltpu.VMEM((2, 2 * cy, cz), bf16),
            pltpu.VMEM((2, 4, STEPS // 2, 2 * cy, cz), bf16),
            pltpu.VMEM((2, 4, planes // 4, 2 * cy, cz), bf16),
            pltpu.VMEM((2, 3, 2, 2 * cy, cz), bf16),
            pltpu.VMEM((2, 2, 3, 2 * cy, cz), bf16),
            pltpu.VMEM((8, cz), f32),
            pltpu.VMEM((4 * cz, hmax), bf16),
            pltpu.VMEM((cx * cy // 4, hmax), f32),
            pltpu.VMEM((STEPS, tiles // 2, 16, row_tile), jnp.bfloat16),
            pltpu.VMEM(radiation.shape, jnp.bfloat16),
            pltpu.VMEM((groups, owned * STEPS, row_tile), f32),
            pltpu.SemaphoreType.DMA((len(MESSAGES),)),
            pltpu.SemaphoreType.DMA((len(MESSAGES),)),
            pltpu.SemaphoreType.DMA((STEPS, n_af)),
            pltpu.SemaphoreType.DMA((STEPS, n_af)),
            pltpu.SemaphoreType.DMA((groups,)),
            pltpu.SemaphoreType.DMA((groups,)),
            pltpu.SemaphoreType.DMA((8,)),
            pltpu.SemaphoreType.DMA((2,)),
        ],
        compiler_params=pltpu.CompilerParams(
            collective_id=0, has_side_effects=True, vmem_limit_bytes=24 * 1024 * 1024
        ),
    )(*operands)
    return pl.pallas_call(
        finish,
        out_shape=out_shape,
        in_specs=[anyw] * 3,
        out_specs=(hbm,) * 3,
        scratch_shapes=[pltpu.SemaphoreType.DMA((3,))],
        compiler_params=pltpu.CompilerParams(vmem_limit_bytes=16 * 1024 * 1024),
    )(*results)


def solution(mesh):
    placed = (
        P(None, "gx", "gy", "af"),
        P("gx", "gy", "af"),
        P(),
        P(),
        P("gx", "gy", "af"),
        P("gx", "gy", "af", None),
        P(("gx", "gy"), "af", None),
        P("af", ("gx", "gy"), None, None, None, None),
    )
    sizes = (mesh.shape["gx"], mesh.shape["gy"], mesh.shape["af"])
    return jax.shard_map(
        functools.partial(on_device, sizes),
        mesh=mesh,
        in_specs=placed,
        out_specs=(P(None, "gx", "gy", "af"), P(None, "gx", "gy", "af"), P(None, "af")),
        check_vma=False,
    )
```
